32 devices in a mesh: row: 8 (over z, x), col: 4 (over y, core).
Axes of the slice: x: 2, y: 2, z: 4, core: 2. Of those that a mesh axis runs over, the one named last changes fastest.
Arguments:
- feats: bfloat16 [4096, 1024], P(('row', 'col')), may hold values from -6 to 6
- weight: bfloat16 [1024, 1024], replicated, may hold values from -0.1875 to 0.1875
- tile_vals: bfloat16 [8, 4, 32, 128, 128], P('row', 'col'), may hold values from -0.25 to 0.25
- tile_rows: int32 [8, 4, 32], P('row', 'col'), may hold values from 0 to 3, as said below
- tile_cols: int32 [8, 4, 32], P('row', 'col'), may hold values from 0 to 7
- tile_count: int32 [8, 4], P('row', 'col'), may hold values from 4 to 32, as said below
- grad_out: bfloat16 [4096, 1024], P(('row', 'col')), may hold values from -6 to 6
Outputs:
- activated: bfloat16 [4096, 1024], P(('row', 'col'))
- grad_feats: bfloat16 [4096, 1024], P(('row', 'col'))
- grad_weight: float32 [1024, 1024], replicated
The draws below stay inside these ranges and needn't reach their ends.
Inputs may be any that keep to these rules, and one draw needn't show every extreme that they name: On each grid block the 32 slots name distinct tile positions (tile_rows, tile_cols); only the first tile_count slots are live. `tile_count`: some grid block has all 32 slots live.
All inputs are finite; a program needn't handle non-finite values.
Results may differ from the reference program's by a relative error of at most 0.029.
Values may be sent and summed in bfloat16 or wider, within the bound.
No kernel may reach another device: no remote copies, remote signals or barrier semaphores. Data moves between devices by JAX's collectives and lax.ppermute only.
A program may use at most 128 MiB of HBM per device.

```python
import jax
import jax.numpy as jnp
from jax import lax

F = 1024
G = 1024
TILE = 128
NODES_DEV = 128
GRID_ROWS = 8
GRID_COLS = 4
NODES = 4096
TROWS = 4
TCOLS = 8
TILES = 32


def tile_pattern(key):
    keys = jax.random.split(key, GRID_ROWS * GRID_COLS)
    orders = jax.vmap(lambda single: jax.random.permutation(single, TROWS * TCOLS))(keys)
    return orders.reshape(GRID_ROWS, GRID_COLS, TILES).astype(jnp.int32)


def draw_tile_rows(key, part):
    return (tile_pattern(jax.random.fold_in(key, 7)) // TCOLS).astype(jnp.int32)


def draw_tile_cols(key, part):
    return (tile_pattern(jax.random.fold_in(key, 7)) % TCOLS).astype(jnp.int32)


def draw_tile_count(key, part):
    first_key, second_key = jax.random.split(jax.random.fold_in(key, 11))
    lowest = max(1, TILES // 8)
    highest = max(lowest + 1, TILES * 5 // 8)
    counts = jax.random.randint(first_key, (GRID_ROWS * GRID_COLS,), lowest, highest, dtype=jnp.int32)
    chosen = jax.random.randint(second_key, (), 0, GRID_ROWS * GRID_COLS, dtype=jnp.int32)
    positions = jnp.arange(GRID_ROWS * GRID_COLS, dtype=jnp.int32)
    counts = jnp.where(positions == chosen, jnp.int32(TILES), counts)
    return counts.reshape(GRID_ROWS, GRID_COLS).astype(jnp.int32)


def level_of(rng, extent, cuts, low, largest):
    gain = 1.0
    for axis_at, blocks in cuts:
        draws = jax.random.uniform(jax.random.fold_in(jax.random.fold_in(rng, 6), axis_at), (blocks,), jnp.float32, low / len(cuts), largest / len(cuts))
        gain = gain * jnp.repeat(jnp.exp(draws), extent[axis_at] // blocks).reshape((-1,) + (1,) * (len(extent) - 1 - axis_at))
    return gain


def normal_values(own_key, dims, scale, bound, cuts=(), held_as=jnp.bfloat16):
    values = jax.random.normal(own_key, dims, jnp.float32) * scale
    if len(cuts) > 0:
        values = level_of(own_key, dims, cuts, -0.22, 0.18) * values
    return jnp.clip(values, min=-bound, max=bound).astype(held_as)


def setup_inputs(seed: int = 0) -> dict:
    arg_keys = jax.random.split(jax.random.key(seed), 8)
    return {
        "feats": normal_values(arg_keys[0], (NODES, F), 1.0, 6.0, ((0, 32),)),
        "weight": normal_values(arg_keys[1], (F, G), F ** -0.5, 0.1875),
        "tile_vals": normal_values(arg_keys[2], (GRID_ROWS, GRID_COLS, TILES, TILE, TILE), (TCOLS * TILE // 2) ** -0.5, 0.25, ((0, 8), (1, 4))),
        "tile_rows": draw_tile_rows(jax.random.fold_in(arg_keys[7], 71), 0),
        "tile_cols": draw_tile_cols(jax.random.fold_in(arg_keys[7], 71), 0),
        "tile_count": draw_tile_count(jax.random.fold_in(arg_keys[7], 71), 0),
        "grad_out": normal_values(arg_keys[6], (NODES, G), 1.0, 6.0, ((0, 32),)),
    }


def round_half(value):
    return lax.optimization_barrier(value.astype(jnp.bfloat16)).astype(jnp.float32)


def block_terms(block_vals, block_rows, block_cols, live_count, source, out_tiles, transpose):
    slots = block_vals.shape[0]
    vals_wide = block_vals.astype(jnp.float32)
    if transpose:
        picked = source[block_rows].astype(jnp.float32)
        products = jnp.einsum("tba,tbf->taf", vals_wide, picked)
        target = block_cols
    else:
        picked = source[block_cols].astype(jnp.float32)
        products = jnp.einsum("tab,tbf->taf", vals_wide, picked)
        target = block_rows
    active = jnp.arange(slots, dtype=jnp.int32) < live_count
    placer = ((target[None, :] == jnp.arange(out_tiles, dtype=jnp.int32)[:, None]) & active[None, :]).astype(jnp.float32)
    return jnp.einsum("rt,taf->raf", placer, products, precision=lax.Precision.HIGHEST)


def apply_adjacency(source, tile_vals, tile_rows, tile_cols, tile_count, transpose):
    grid_r, grid_c = tile_count.shape
    width = source.shape[1]
    flat_vals = tile_vals.reshape(grid_r * grid_c, TILES, TILE, TILE)
    flat_rows = tile_rows.reshape(grid_r * grid_c, TILES)
    flat_cols = tile_cols.reshape(grid_r * grid_c, TILES)
    flat_count = tile_count.reshape(grid_r * grid_c)
    if transpose:
        row_blocks = source.reshape(grid_r, TROWS, TILE, width)
        running = jnp.zeros((grid_r, grid_c, NODES_DEV, width), jnp.float32)
    else:
        node_blocks = source.reshape(grid_r, grid_c, NODES_DEV, width)
        running = jnp.zeros((grid_r, TROWS, TILE, width), jnp.float32)

    def visit(number, running):
        i_idx = number // grid_c
        j_idx = number % grid_c
        if transpose:
            tiles_in = jnp.take(row_blocks, i_idx, axis=0)
            part = block_terms(flat_vals[number], flat_rows[number], flat_cols[number], flat_count[number], tiles_in, TCOLS, True)
            part = round_half(part.reshape(grid_r, NODES_DEV, width))
            current = jnp.take(running, j_idx, axis=1)
            return lax.dynamic_update_index_in_dim(running, current + part, j_idx, 1)
        tiles_in = jnp.take(node_blocks, j_idx, axis=1).reshape(TCOLS, TILE, width)
        part = block_terms(flat_vals[number], flat_rows[number], flat_cols[number], flat_count[number], tiles_in, TROWS, False)
        part = round_half(part)
        current = jnp.take(running, i_idx, axis=0)
        return lax.dynamic_update_index_in_dim(running, current + part, i_idx, 0)

    running = lax.fori_loop(0, grid_r * grid_c, visit, running)
    return running.reshape(NODES, width)


def reference(feats, weight, tile_vals, tile_rows, tile_cols, tile_count, grad_out):
    aggregated = apply_adjacency(feats, tile_vals, tile_rows, tile_cols, tile_count, False).astype(jnp.bfloat16)
    pre_act = jnp.dot(aggregated, weight, preferred_element_type=jnp.float32)
    activated = jax.nn.silu(pre_act).astype(jnp.bfloat16)
    sigmoid_val = jax.nn.sigmoid(pre_act)
    slope_val = sigmoid_val * (1.0 + pre_act * (1.0 - sigmoid_val))
    grad_pre = (grad_out.astype(jnp.float32) * slope_val).astype(jnp.bfloat16)
    grad_weight = jnp.dot(aggregated.T, grad_pre, preferred_element_type=jnp.float32)
    back_rows = jnp.dot(grad_pre, weight.T, preferred_element_type=jnp.float32).astype(jnp.bfloat16)
    grad_feats = apply_adjacency(back_rows, tile_vals, tile_rows, tile_cols, tile_count, True).astype(jnp.bfloat16)
    return (activated, grad_feats, grad_weight)
```

```python
import functools

import jax
import jax.numpy as jnp
from jax import lax
from jax.experimental import pallas as pl
from jax.experimental.pallas import tpu as pltpu
from jax.sharding import PartitionSpec as P

CHUNKS = 2
VMEM_LIMIT = 48 * 1024 * 1024


def ring_of(count, width):
    height = count // width
    if count % width or width % 2 or height < 2:
        return list(range(count))
    walk = [(0, x) for x in range(width)]
    for turn, x in enumerate(reversed(range(width))):
        down = range(1, height) if turn % 2 == 0 else range(height - 1, 0, -1)
        walk += [(z, x) for z in down]
    return [z * width + x for z, x in walk]


def vmem_call(kernel, out_shapes, scratch=(), smem=0, inputs=0, flops=0, moved=0):
    specs = [pl.BlockSpec(memory_space=pltpu.SMEM)] * smem + [pl.BlockSpec(memory_space=pltpu.VMEM)] * inputs
    return pl.pallas_call(
        kernel,
        out_shape=out_shapes,
        in_specs=specs,
        out_specs=jax.tree.map(lambda _: pl.BlockSpec(memory_space=pltpu.VMEM), out_shapes),
        scratch_shapes=list(scratch),
        compiler_params=pltpu.CompilerParams(vmem_limit_bytes=VMEM_LIMIT),
        cost_estimate=pl.CostEstimate(flops=flops, bytes_accessed=moved, transcendentals=0),
    )


def place_tiles(vals, row_at, col_at, live, rows, cols):
    side = vals.shape[1]

    def kernel(row_ref, col_ref, live_ref, vals_ref, out_ref):
        out_ref[...] = jnp.zeros_like(out_ref)

        def put(slot, carry):
            top = pl.multiple_of(row_ref[slot] * side, side)
            left = pl.multiple_of(col_ref[slot] * side, side)
            out_ref[pl.ds(top, side), pl.ds(left, side)] = vals_ref[slot]
            return carry

        lax.fori_loop(0, live_ref[0], put, 0)

    shape = jax.ShapeDtypeStruct((rows * side, cols * side), vals.dtype)
    call = vmem_call(kernel, shape, smem=3, inputs=1, moved=2 * vals.size * 2)
    return call(row_at, col_at, live, vals)


def aggregate(adjacency, pieces, ends):
    rows, depth = adjacency.shape
    height, width = pieces[0].shape
    half = rows // 2

    def kernel(*refs):
        adj_ref = refs[0]
        piece_refs = refs[1 : 1 + len(pieces)]
        right_ref, left_ref, near_ref, far_ref, held = refs[1 + len(pieces) :]
        for place, piece_ref in enumerate(piece_refs):
            held[place * height : (place + 1) * height] = piece_ref[...]
        held[depth - height :, : width // 2] = right_ref[...]
        held[depth - height :, width // 2 :] = left_ref[...]
        far_ref[...] = jnp.dot(adj_ref[half:], held[...], preferred_element_type=jnp.float32).astype(jnp.bfloat16)
        near_ref[...] = jnp.dot(adj_ref[:half], held[...], preferred_element_type=jnp.float32)

    shapes = (
        jax.ShapeDtypeStruct((half, width), jnp.float32),
        jax.ShapeDtypeStruct((half, width), jnp.bfloat16),
    )
    call = vmem_call(
        kernel,
        shapes,
        scratch=[pltpu.VMEM((depth, width), jnp.bfloat16)],
        inputs=3 + len(pieces),
        flops=2 * rows * depth * width,
        moved=2 * (rows * depth + depth * width + rows * width),
    )
    return call(adjacency, *pieces, *ends)


def dense(where, held, arrived, weight, cotangents):
    chunks = len(held)
    rows, width = held[0].shape
    depth, cols = weight.shape
    groups = len(cotangents)
    side = rows // groups
    part = depth // groups
    quarter = part // 2

    def kernel(*refs):
        refs = list(refs)
        where_ref = refs.pop(0)
        held_refs = [refs.pop(0) for _ in range(chunks)]
        arrived_refs = [[refs.pop(0) for _ in range(chunks)] for _ in range(groups - 1)]
        weight_ref = refs.pop(0)
        cot_refs = [refs.pop(0) for _ in range(groups)]
        act_ref, near_ref, far_ref = refs[:3]
        back_refs = refs[3 : 3 + chunks]
        agg = refs[-2]
        grad = refs[-1]
        for h in range(chunks):
            for g in range(groups):
                total = held_refs[h][g * side : (g + 1) * side].astype(jnp.float32)
                for s in range(1, groups):
                    at = (g + s) % groups
                    total = total + arrived_refs[s - 1][h][at * side : (at + 1) * side].astype(jnp.float32)
                agg[g * side : (g + 1) * side, h * width : (h + 1) * width] = total.astype(jnp.bfloat16)
        for g in range(groups):
            value = jnp.dot(agg[g * side : (g + 1) * side], weight_ref[...], preferred_element_type=jnp.float32)
            gate = jax.nn.sigmoid(value)
            if g == 0:
                act_ref[...] = (value * gate).astype(jnp.bfloat16)
            slope = gate * (1.0 + value * (1.0 - gate))
            cot = cot_refs[(groups - g) % groups][...].astype(jnp.float32)
            grad[g * side : (g + 1) * side] = (cot * slope).astype(jnp.bfloat16)
        for h in range(chunks):
            back_refs[h][...] = lax.dot_general(
                grad[...], weight_ref[h * width : (h + 1) * width], (((1,), (1,)), ((), ())), preferred_element_type=jnp.float32
            ).astype(jnp.bfloat16)
        first = where_ref[0] * part
        near_at = pl.multiple_of(first + where_ref[1] * quarter, 128)
        far_at = pl.multiple_of(first + (1 - where_ref[1]) * quarter, 128)
        far_ref[...] = lax.dot_general(
            agg[:, pl.ds(far_at, quarter)], grad[...], (((0,), (0,)), ((), ())), preferred_element_type=jnp.float32
        ).astype(jnp.bfloat16)
        near_ref[...] = lax.dot_general(
            agg[:, pl.ds(near_at, quarter)], grad[...], (((0,), (0,)), ((), ())), preferred_element_type=jnp.float32
        )

    shapes = [
        jax.ShapeDtypeStruct((side, cols), jnp.bfloat16),
        jax.ShapeDtypeStruct((quarter, cols), jnp.float32),
        jax.ShapeDtypeStruct((quarter, cols), jnp.bfloat16),
    ] + [jax.ShapeDtypeStruct((rows, width), jnp.bfloat16)] * chunks
    call = vmem_call(
        kernel,
        shapes,
        scratch=[pltpu.VMEM((rows, depth), jnp.bfloat16), pltpu.VMEM((rows, cols), jnp.bfloat16)],
        smem=1,
        inputs=chunks * groups + 1 + groups,
        flops=2 * rows * cols * (2 * depth + part),
        moved=2 * (depth * cols + 6 * rows * depth),
    )
    outs = call(where, *held, *[a for step in arrived for a in step], weight, *cotangents)
    return outs[0], outs[1], outs[2], outs[3:]


def back_blocks(adjacency, near, far, count):
    rows, depth = adjacency.shape
    half, width = near.shape
    height = depth // count

    def kernel(adj_ref, near_ref, far_ref, *out_refs):
        held = out_refs[-1]
        held[:half] = near_ref[...]
        held[half:] = far_ref[...]
        for place in reversed(range(count)):
            block = lax.dot_general(
                adj_ref[:, place * height : (place + 1) * height],
                held[...],
                (((0,), (0,)), ((), ())),
                preferred_element_type=jnp.float32,
            ).astype(jnp.bfloat16)
            if place == count - 1:
                out_refs[place][...] = block[:, : width // 2]
                out_refs[place + 1][...] = block[:, width // 2 :]
            else:
                out_refs[place][...] = block

    shapes = [jax.ShapeDtypeStruct((height, width), jnp.bfloat16)] * (count - 1)
    shapes += [jax.ShapeDtypeStruct((height, width // 2), jnp.bfloat16)] * 2
    call = vmem_call(
        kernel,
        shapes,
        scratch=[pltpu.VMEM((rows, width), jnp.bfloat16)],
        inputs=3,
        flops=2 * rows * depth * width,
        moved=2 * (rows * depth + depth * width + rows * width),
    )
    return call(adjacency, near, far)


def weight_blocks(where, near, arrived, count):
    rows, cols = near.shape
    height = rows // count

    def kernel(where_ref, near_ref, arrived_ref, *out_refs):
        for place in range(count):
            step = (place + 1) // 2
            away = step if place % 2 == 0 or place == count - 1 else count - step
            at = pl.multiple_of(lax.rem(where_ref[0] + away, count) * height, height)
            block = near_ref[pl.ds(at, height)] + arrived_ref[pl.ds(at, height)].astype(jnp.float32)
            block = block.astype(jnp.bfloat16)
            if place == count - 1:
                out_refs[place][...] = block[:, : cols // 2]
                out_refs[place + 1][...] = block[:, cols // 2 :]
            else:
                out_refs[place][...] = block

    shapes = [jax.ShapeDtypeStruct((height, cols), jnp.bfloat16)] * (count - 1)
    shapes += [jax.ShapeDtypeStruct((height, cols // 2), jnp.bfloat16)] * 2
    call = vmem_call(kernel, shapes, smem=1, inputs=2, flops=rows * cols, moved=8 * rows * cols)
    return call(where, near, arrived)


def add_pair(right, left, from_left, from_right, halves):
    height, width = right.shape

    def kernel(right_ref, left_ref, first_ref, second_ref, out_right, out_left):
        if halves:
            middle = width // 2
            out_right[:, middle:] = right_ref[:, middle:]
            out_right[:, :middle] = right_ref[:, :middle] + first_ref[...]
            out_left[:, :middle] = left_ref[:, :middle]
            out_left[:, middle:] = left_ref[:, middle:] + second_ref[...]
        else:
            out_right[...] = right_ref[...] + first_ref[...]
            out_left[...] = left_ref[...] + second_ref[...]

    shapes = (jax.ShapeDtypeStruct(right.shape, right.dtype),) * 2
    call = vmem_call(kernel, shapes, inputs=4, flops=2 * right.size, moved=12 * right.size)
    return call(right, left, from_left, from_right)


def join_ring(where, pieces, ends, count):
    height, cols = pieces[0].shape

    def kernel(where_ref, *refs):
        out_ref = refs[-1]
        for place in range(count):
            step = (place + 1) // 2
            away = step if place % 2 == 0 or place == count - 1 else count - step
            at = pl.multiple_of(lax.rem(where_ref[0] + away, count) * height, height)
            if place == count - 1:
                out_ref[pl.ds(at, height), : cols // 2] = refs[place][...]
                out_ref[pl.ds(at, height), cols // 2 :] = refs[place + 1][...]
            else:
                out_ref[pl.ds(at, height)] = refs[place][...]

    shape = jax.ShapeDtypeStruct((height * count, cols), pieces[0].dtype)
    call = vmem_call(kernel, shape, smem=1, inputs=len(pieces) + 2, moved=4 * height * count * cols)
    return call(where, *pieces, *ends)


def join_weight(where, near, far):
    quarter, cols = near[0].shape
    groups = len(near)

    def kernel(where_ref, *refs):
        out_ref = refs[-1]
        for s in range(groups):
            group = lax.rem(where_ref[0] + groups - s, groups)
            for other in range(2):
                core = where_ref[1] if other == 0 else 1 - where_ref[1]
                at = pl.multiple_of((group * 2 + core) * quarter, quarter)
                out_ref[pl.ds(at, quarter)] = refs[other * groups + s][...].astype(jnp.float32)

    shape = jax.ShapeDtypeStruct((quarter * 2 * groups, cols), jnp.float32)
    call = vmem_call(kernel, shape, smem=1, inputs=2 * groups, moved=12 * quarter * groups * cols)
    return call(where, *near, *far)


def body(width, feats, weight, tile_vals, tile_rows, tile_cols, tile_count, grad_out):
    side = tile_vals.shape[-1]
    count = lax.axis_size("row")
    columns = lax.axis_size("col")
    groups = columns // 2
    ring = ring_of(count, width)
    spot = [0] * count
    for place, row in enumerate(ring):
        spot[row] = place
    spot = jnp.array(spot, jnp.int32)
    me = spot[lax.axis_index("row")]
    core = lax.axis_index("col") % 2
    group = lax.axis_index("col") // 2

    to_right = [(ring[k], ring[(k + 1) % count]) for k in range(count)]
    to_left = [(ring[k], ring[(k - 1) % count]) for k in range(count)]
    swap = [(k, k ^ 1) for k in range(columns)]

    def go_right(value):
        return lax.ppermute(value, "row", to_right)

    def go_left(value):
        return lax.ppermute(value, "row", to_left)

    def swap_core(value):
        return lax.ppermute(value, "col", swap)

    def from_group(value, steps):
        return lax.ppermute(value, "col", [(k, (k + 2 * steps) % columns) for k in range(columns)])

    def gather_ring(piece):
        pieces = [piece]
        right = left = piece
        for _ in range(count // 2 - 1):
            right, left = go_right(right), go_left(left)
            pieces += [right, left]
        middle = piece.shape[1] // 2
        return pieces, [go_right(right[:, :middle]), go_left(left[:, middle:])]

    def scatter_ring(blocks):
        right, left = go_right(blocks[count - 1]), go_left(blocks[count])
        for step in range(count // 2 - 1, 0, -1):
            right, left = add_pair(blocks[2 * step], blocks[2 * step - 1], right, left, step == count // 2 - 1)
            right, left = go_right(right), go_left(left)
        return (blocks[0].astype(jnp.float32) + right.astype(jnp.float32) + left.astype(jnp.float32)).astype(jnp.bfloat16)

    rows = tile_rows[0, 0]
    row_at = (rows % 2 ^ core) * groups + (rows // 2 - group) % groups
    away = (spot[tile_cols[0, 0]] - me) % count
    col_at = jnp.where(away < count // 2, 2 * away, 2 * (count - away) - 1)
    adjacency = place_tiles(tile_vals[0, 0], row_at, col_at, tile_count[0], columns, count)

    chunk = feats.shape[1] // CHUNKS
    cotangents = [grad_out] + [from_group(grad_out, s) for s in range(1, groups)]
    held = []
    arrived = [[] for _ in range(groups - 1)]
    for h in range(CHUNKS):
        pieces, ends = gather_ring(feats[:, h * chunk : (h + 1) * chunk])
        near, far = aggregate(adjacency, pieces, ends)
        total = (near + swap_core(far).astype(jnp.float32)).astype(jnp.bfloat16)
        held.append(total)
        for s in range(1, groups):
            arrived[s - 1].append(from_group(total, s))

    where = jnp.stack([group, core]).astype(jnp.int32)
    activated, near_weight, far_weight, back = dense(where, held, arrived, weight, cotangents)

    place = me.reshape(1).astype(jnp.int32)
    terms = weight_blocks(place, near_weight, swap_core(far_weight), count)
    own = scatter_ring(terms)
    pieces, ends = gather_ring(own)
    near_quarters = [join_ring(place, pieces, ends, count)]
    near_quarters += [from_group(near_quarters[0], s) for s in range(1, groups)]
    far_quarters = [swap_core(q) for q in near_quarters]
    grad_weight = join_weight(where, near_quarters, far_quarters)

    grads = []
    for h in range(CHUNKS):
        blocks = back_blocks(adjacency, back[h], swap_core(back[h]), count)
        grads.append(scatter_ring(blocks))
    grad_feats = jnp.concatenate(grads, axis=1)
    return (activated, grad_feats, grad_weight)


def solution(mesh):
    spread = {d.coords[0] for d in mesh.devices.flat if hasattr(d, "coords")}
    placed = (
        P(("row", "col"), None),
        P(),
        P("row", "col", None, None, None),
        P("row", "col", None),
        P("row", "col", None),
        P("row", "col"),
        P(("row", "col"), None),
    )
    return jax.shard_map(
        functools.partial(body, max(1, len(spread))),
        mesh=mesh,
        in_specs=placed,
        out_specs=(P(("row", "col"), None), P(("row", "col"), None), P()),
        check_vma=False,
    )
```

```python
import functools

import jax
import jax.numpy as jnp
from jax import lax
from jax.experimental import pallas as pl
from jax.experimental.pallas import tpu as pltpu
from jax.sharding import PartitionSpec as P

CHUNKS = 2
VMEM_LIMIT = 48 * 1024 * 1024


def ring_of(count, width):
    height = count // width
    if count % width or width % 2 or height < 2:
        return list(range(count))
    walk = [(0, x) for x in range(width)]
    for turn, x in enumerate(reversed(range(width))):
        down = range(1, height) if turn % 2 == 0 else range(height - 1, 0, -1)
        walk += [(z, x) for z in down]
    return [z * width + x for z, x in walk]


def ring_slots(count):
    return [0] + [away for step in range(1, count // 2) for away in (count - step, step)] + [count // 2]


def pick(index, table):
    value = jnp.int32(table[0])
    for at in range(1, len(table)):
        value = jnp.where(index == at, jnp.int32(table[at]), value)
    return value


def position(spot):
    column = lax.axis_index("col")
    return pick(lax.axis_index("row"), spot), lax.div(column, jnp.int32(2)), lax.rem(column, jnp.int32(2))


class Tiling:
    def __init__(self, rows, cols, count):
        self.split = max(1, 16 * count // rows)
        self.height = rows * self.split // count
        self.width = cols // self.split
        self.shape = (self.height, self.width)

    def at(self, block, base=0):
        top = pl.multiple_of(base + lax.div(block, jnp.int32(self.split)) * self.height, self.height)
        if self.split == 1:
            return pl.ds(top, self.height), slice(None)
        return pl.ds(top, self.height), pl.ds(pl.multiple_of(lax.rem(block, jnp.int32(self.split)) * self.width, 128), self.width)


def vmem_call(kernel, out_shapes, args, scratch=(), smem=0, hbm=0, hbm_out=False, after=(), flops=0, moved=0):
    vmem = pl.BlockSpec(memory_space=pltpu.VMEM)
    anywhere = pl.BlockSpec(memory_space=pl.ANY)
    specs = [pl.BlockSpec(memory_space=pltpu.SMEM)] * smem + [anywhere] * hbm
    specs += [vmem] * (len(args) - smem - hbm) + [anywhere] * len(after)
    count = len(args)

    def inner(*refs):
        kernel(*refs[:count], *refs[count + len(after) :])

    return pl.pallas_call(
        inner,
        out_shape=out_shapes,
        in_specs=specs,
        out_specs=jax.tree.map(lambda _: anywhere if hbm_out else vmem, out_shapes),
        scratch_shapes=list(scratch),
        compiler_params=pltpu.CompilerParams(vmem_limit_bytes=VMEM_LIMIT),
        cost_estimate=pl.CostEstimate(flops=flops, bytes_accessed=moved, transcendentals=0),
    )(*args, *after)


def place_tiles(spot, groups, vals, tile_rows, tile_cols, tile_count, feats, first):
    slots, side = vals.shape[2], vals.shape[-1]
    count = len(spot)

    def kernel(row_ref, col_ref, live_ref, vals_hbm, feats_hbm, out_ref, rest_ref, held, sems):
        feats_copy = pltpu.make_async_copy(feats_hbm.at[:, first:], rest_ref, sems.at[0])
        feats_copy.start()
        vals_copy = pltpu.make_async_copy(vals_hbm.at[0, 0], held, sems.at[1])
        vals_copy.start()
        me, group, core = position(spot)
        out_ref[...] = jnp.zeros_like(out_ref)
        vals_copy.wait()

        def put(slot, carry):
            row = row_ref[0, 0, slot]
            other = lax.rem(row, 2) ^ core
            along = lax.rem(lax.div(row, 2) + groups - group, groups)
            top = pl.multiple_of((other * groups + along) * side, side)
            away = lax.rem(pick(col_ref[0, 0, slot], spot) + count - me, count)
            col = jnp.where(away < count // 2, 2 * away, 2 * (count - away) - 1)
            left = pl.multiple_of(col * side, side)
            out_ref[pl.ds(top, side), pl.ds(left, side)] = held[slot]
            return carry

        lax.fori_loop(0, live_ref[0, 0], put, 0)
        feats_copy.wait()

    shapes = (
        jax.ShapeDtypeStruct((2 * groups * side, count * side), vals.dtype),
        jax.ShapeDtypeStruct((feats.shape[0], feats.shape[1] - first), feats.dtype),
    )
    scratch = [pltpu.VMEM((slots, side, side), vals.dtype), pltpu.SemaphoreType.DMA((2,))]
    args = (tile_rows, tile_cols, tile_count, vals, feats)
    return vmem_call(kernel, shapes, args, scratch=scratch, smem=3, hbm=2, moved=4 * vals.size)


def aggregate(adjacency, pieces, ends, after):
    rows, depth = adjacency.shape
    height, width = pieces[0].shape
    half = rows // 2

    def kernel(*refs):
        adj_ref = refs[0]
        piece_refs = refs[1 : 1 + len(pieces)]
        right_ref, left_ref, near_ref, far_ref, held = refs[1 + len(pieces) :]
        for place, piece_ref in enumerate(piece_refs):
            held[place * height : (place + 1) * height] = piece_ref[...]
        held[depth - height :, : width // 2] = right_ref[...]
        held[depth - height :, width // 2 :] = left_ref[...]
        far_ref[...] = jnp.dot(adj_ref[half:], held[...], preferred_element_type=jnp.float32).astype(jnp.bfloat16)
        near_ref[...] = jnp.dot(adj_ref[:half], held[...], preferred_element_type=jnp.float32)

    shapes = (
        jax.ShapeDtypeStruct((half, width), jnp.float32),
        jax.ShapeDtypeStruct((half, width), jnp.bfloat16),
    )
    return vmem_call(
        kernel,
        shapes,
        (adjacency, *pieces, *ends),
        scratch=[pltpu.VMEM((depth, width), jnp.bfloat16)],
        after=after,
        flops=2 * rows * depth * width,
        moved=2 * (rows * depth + depth * width + rows * width),
    )


def dense(spot, held, arrived, weight, cotangents):
    chunks = len(held)
    rows, width = held[0].shape
    depth, cols = weight.shape
    groups = len(cotangents)
    side = rows // groups
    part = depth // groups
    quarter = part // 2

    def kernel(*refs):
        refs = list(refs)
        _, group, core = position(spot)
        held_refs = [refs.pop(0) for _ in range(chunks)]
        arrived_refs = [[refs.pop(0) for _ in range(chunks)] for _ in range(groups - 1)]
        weight_ref = refs.pop(0)
        cot_refs = [refs.pop(0) for _ in range(groups)]
        act_ref, near_ref, far_ref = refs[:3]
        back_refs = refs[3 : 3 + chunks]
        agg = refs[-2]
        grad = refs[-1]
        for h in range(chunks):
            for g in range(groups):
                total = held_refs[h][g * side : (g + 1) * side].astype(jnp.float32)
                for s in range(1, groups):
                    at = (g + s) % groups
                    total = total + arrived_refs[s - 1][h][at * side : (at + 1) * side].astype(jnp.float32)
                agg[g * side : (g + 1) * side, h * width : (h + 1) * width] = total.astype(jnp.bfloat16)
        for g in range(groups):
            value = jnp.dot(agg[g * side : (g + 1) * side], weight_ref[...], preferred_element_type=jnp.float32)
            gate = jax.nn.sigmoid(value)
            if g == 0:
                act_ref[...] = (value * gate).astype(jnp.bfloat16)
            slope = gate * (1.0 + value * (1.0 - gate))
            cot = cot_refs[(groups - g) % groups][...].astype(jnp.float32)
            grad[g * side : (g + 1) * side] = (cot * slope).astype(jnp.bfloat16)
        for h in range(chunks):
            back_refs[h][...] = lax.dot_general(
                grad[...], weight_ref[h * width : (h + 1) * width], (((1,), (1,)), ((), ())), preferred_element_type=jnp.float32
            ).astype(jnp.bfloat16)
        first = group * part
        near_at = pl.multiple_of(first + core * quarter, 128)
        far_at = pl.multiple_of(first + (1 - core) * quarter, 128)
        far_ref[...] = lax.dot_general(
            agg[:, pl.ds(far_at, quarter)], grad[...], (((0,), (0,)), ((), ())), preferred_element_type=jnp.float32
        ).astype(jnp.bfloat16)
        near_ref[...] = lax.dot_general(
            agg[:, pl.ds(near_at, quarter)], grad[...], (((0,), (0,)), ((), ())), preferred_element_type=jnp.float32
        )

    shapes = [
        jax.ShapeDtypeStruct((side, cols), jnp.bfloat16),
        jax.ShapeDtypeStruct((quarter, cols), jnp.float32),
        jax.ShapeDtypeStruct((quarter, cols), jnp.bfloat16),
    ] + [jax.ShapeDtypeStruct((rows, width), jnp.bfloat16)] * chunks
    outs = vmem_call(
        kernel,
        shapes,
        (*held, *[a for step in arrived for a in step], weight, *cotangents),
        scratch=[pltpu.VMEM((rows, depth), jnp.bfloat16), pltpu.VMEM((rows, cols), jnp.bfloat16)],
        flops=2 * rows * cols * (2 * depth + part),
        moved=2 * (depth * cols + 6 * rows * depth),
    )
    return outs[0], outs[1], outs[2], outs[3:]


def back_blocks(adjacency, near, far, count):
    rows, depth = adjacency.shape
    half, width = near.shape
    height = depth // count

    def kernel(adj_ref, near_ref, far_ref, *out_refs):
        held = out_refs[-1]
        held[:half] = near_ref[...]
        held[half:] = far_ref[...]
        for place in reversed(range(count)):
            block = lax.dot_general(
                adj_ref[:, place * height : (place + 1) * height],
                held[...],
                (((0,), (0,)), ((), ())),
                preferred_element_type=jnp.float32,
            ).astype(jnp.bfloat16)
            if place == count - 1:
                out_refs[place][...] = block[:, : width // 2]
                out_refs[place + 1][...] = block[:, width // 2 :]
            else:
                out_refs[place][...] = block

    shapes = [jax.ShapeDtypeStruct((height, width), jnp.bfloat16)] * (count - 1)
    shapes += [jax.ShapeDtypeStruct((height, width // 2), jnp.bfloat16)] * 2
    return vmem_call(
        kernel,
        shapes,
        (adjacency, near, far),
        scratch=[pltpu.VMEM((rows, width), jnp.bfloat16)],
        flops=2 * rows * depth * width,
        moved=2 * (rows * depth + depth * width + rows * width),
    )


def weight_blocks(spot, near, arrived, tiling):
    count = len(spot)
    middle = tiling.width // 2

    def kernel(near_ref, arrived_ref, *out_refs):
        me, _, _ = position(spot)
        for place, away in enumerate(ring_slots(count)):
            at = tiling.at(lax.rem(me + away, count))
            block = (near_ref[at] + arrived_ref[at].astype(jnp.float32)).astype(jnp.bfloat16)
            if place == count - 1:
                out_refs[place][...] = block[:, :middle]
                out_refs[place + 1][...] = block[:, middle:]
            else:
                out_refs[place][...] = block

    shapes = [jax.ShapeDtypeStruct(tiling.shape, jnp.bfloat16)] * (count - 1)
    shapes += [jax.ShapeDtypeStruct((tiling.height, middle), jnp.bfloat16)] * 2
    return vmem_call(kernel, shapes, (near, arrived), flops=near.size, moved=8 * near.size)


def add_round(pairs, finals, after=()):
    args = [a for group in pairs + finals for a in group]

    def kernel(*refs):
        ins, outs = list(refs[: len(args)]), list(refs[len(args) :])
        for _ in pairs:
            right, left, first, second = (ins.pop(0) for _ in range(4))
            width, part = right.shape[1], first.shape[1]
            out_right, out_left = outs.pop(0), outs.pop(0)
            out_right[:, :part] = right[:, :part] + first[...]
            out_left[:, width - part :] = left[:, width - part :] + second[...]
            if part < width:
                out_right[:, part:] = right[:, part:]
                out_left[:, : width - part] = left[:, : width - part]
        for _ in finals:
            own, first, second = (ins.pop(0)[...].astype(jnp.float32) for _ in range(3))
            outs.pop(0)[...] = (own + first + second).astype(jnp.bfloat16)

    shapes = [jax.ShapeDtypeStruct(g[0].shape, jnp.bfloat16) for g in pairs for _ in range(2)]
    shapes += [jax.ShapeDtypeStruct(g[0].shape, jnp.bfloat16) for g in finals]
    moved = sum(2 * a.size for a in args)
    outs = vmem_call(kernel, shapes, args, after=after, flops=moved, moved=2 * moved)
    return [tuple(outs[2 * k : 2 * k + 2]) for k in range(len(pairs))], outs[2 * len(pairs) :]


def stack_blocks(blocks, ends):
    height, width = (blocks or ends)[0].shape
    if not blocks:
        width *= 2

    def kernel(*refs):
        out_ref = refs[-1]
        for place in range(len(blocks)):
            out_ref[place * height : (place + 1) * height] = refs[place][...]
        for side in range(len(ends)):
            half = width // 2
            out_ref[len(blocks) * height :, side * half : (side + 1) * half] = refs[len(blocks) + side][...]

    total = len(blocks) + len(ends) // 2
    shape = jax.ShapeDtypeStruct((total * height, width), jnp.bfloat16)
    return vmem_call(kernel, shape, (*blocks, *ends), moved=4 * total * height * width)


def join_weight(spot, groups, tiling, shape, stacks):
    count = len(spot)
    quarter = shape[0] // (2 * groups)
    total = 2 * groups * count

    def kernel(*refs):
        stack_refs, out_ref, wide, sems = refs[: len(stacks)], refs[-3], refs[-2], refs[-1]
        me, group, core = position(spot)
        copies = []
        for ref, (_, aways, steps, other) in zip(stack_refs, stacks):
            back = lax.rem(group + groups - steps, groups)
            base = (back * 2 + (1 - core if other else core)) * quarter
            for place, away in enumerate(aways):
                slot = len(copies)
                wide[slot] = ref[place * tiling.height : (place + 1) * tiling.height].astype(jnp.float32)
                at = tiling.at(lax.rem(me + away, count), base)
                copies.append(pltpu.make_async_copy(wide.at[slot], out_ref.at[at], sems.at[slot]))
                copies[-1].start()
        for copy in copies:
            copy.wait()

    out = jax.ShapeDtypeStruct(shape, jnp.float32)
    scratch = [pltpu.VMEM((total, *tiling.shape), jnp.float32), pltpu.SemaphoreType.DMA((total,))]
    return vmem_call(kernel, out, [s[0] for s in stacks], scratch=scratch, hbm_out=True, moved=6 * shape[0] * shape[1])


def body(width, feats, weight, tile_vals, tile_rows, tile_cols, tile_count, grad_out):
    count = lax.axis_size("row")
    columns = lax.axis_size("col")
    groups = columns // 2
    rounds = count // 2
    ring = ring_of(count, width)
    spot = [0] * count
    for place, row in enumerate(ring):
        spot[row] = place

    to_right = [(ring[k], ring[(k + 1) % count]) for k in range(count)]
    to_left = [(ring[k], ring[(k - 1) % count]) for k in range(count)]
    swap = [(k, k ^ 1) for k in range(columns)]

    def go(right, left):
        return lax.ppermute(right, "row", to_right), lax.ppermute(left, "row", to_left)

    def go_halves(right, left):
        middle = right.shape[1] // 2
        return go(right[:, :middle], left[:, middle:])

    def swap_core(value):
        return lax.ppermute(value, "col", swap)

    def from_group(value, steps):
        return lax.ppermute(value, "col", [(k, (k + 2 * steps) % columns) for k in range(columns)])

    def gather_ring(piece):
        pieces = [piece]
        right = left = piece
        for _ in range(rounds - 1):
            right, left = go(right, left)
            pieces += [right, left]
        return pieces, go_halves(right, left)

    chunk = feats.shape[1] // CHUNKS
    adjacency, second = place_tiles(spot, groups, tile_vals, tile_rows, tile_cols, tile_count, feats, chunk)
    cotangents = [grad_out] + [from_group(grad_out, s) for s in range(1, groups)]
    held = []
    arrived = [[] for _ in range(groups - 1)]
    for h, piece in enumerate((feats[:, :chunk], second)):
        pieces, ends = gather_ring(piece)
        after = cotangents[1:] if h == 0 else [step[0] for step in arrived]
        near, far = aggregate(adjacency, pieces, ends, after)
        total = (near + swap_core(far).astype(jnp.float32)).astype(jnp.bfloat16)
        held.append(total)
        for s in range(1, groups):
            arrived[s - 1].append(from_group(total, s))

    activated, near_weight, far_weight, back = dense(spot, held, arrived, weight, cotangents)

    tiling = Tiling(*near_weight.shape, count)
    blocks = [back_blocks(adjacency, b, swap_core(b), count) for b in back]
    terms = weight_blocks(spot, near_weight, swap_core(far_weight), tiling)
    moving = [None] * CHUNKS
    weight_moving = go(terms[count - 1], terms[count])
    weight_pieces = []
    for slot in range(2 * rounds):
        j, h = divmod(slot, 2)
        pairs, finals, after = [], [], []
        if 0 < slot < rounds:
            step = 2 * (rounds - slot)
            pairs.append((terms[step], terms[step - 1], *weight_moving))
        elif slot == rounds:
            finals.append((terms[0], *weight_moving))
        elif slot > rounds:
            weight_pieces += weight_moving
            after = weight_moving
        if j > 0:
            step = 2 * (rounds - j)
            pairs.append((blocks[h][step], blocks[h][step - 1], *moving[h]))
        sums, ends = add_round(pairs, finals, after) if pairs or finals else ([], [])
        if 0 < slot < rounds:
            weight_moving = go(*sums[0])
        elif slot == rounds:
            weight_pieces.append(ends[0])
            weight_moving = go(ends[0], ends[0])
        elif rounds < slot < 2 * rounds - 1:
            weight_moving = go(*weight_moving)
        elif slot == 2 * rounds - 1:
            weight_moving = go_halves(*weight_moving)
        moving[h] = go(*sums[-1]) if j > 0 else go(blocks[h][count - 1], blocks[h][count])

    _, grads = add_round([], [(blocks[h][0], *moving[h]) for h in range(CHUNKS)])
    grad_feats = jnp.concatenate(grads, axis=1)

    slots = ring_slots(count)
    early = 1 + 2 * (rounds // 2)
    stacks = []
    for first, last in ((0, early), (early, count)):
        stack = stack_blocks(weight_pieces[first:last], weight_moving if last == count else ())
        for s in range(groups):
            value = stack if s == 0 else from_group(stack, s)
            stacks.append((value, slots[first:last], s, False))
            stacks.append((swap_core(value), slots[first:last], s, True))
    grad_weight = join_weight(spot, groups, tiling, weight.shape, stacks)
    return (activated, grad_feats, grad_weight)


def solution(mesh):
    spread = {d.coords[0] for d in mesh.devices.flat if hasattr(d, "coords")}
    placed = (
        P(("row", "col"), None),
        P(),
        P("row", "col", None, None, None),
        P("row", "col", None),
        P("row", "col", None),
        P("row", "col"),
        P(("row", "col"), None),
    )
    return jax.shard_map(
        functools.partial(body, max(1, len(spread))),
        mesh=mesh,
        in_specs=placed,
        out_specs=(P(("row", "col"), None), P(("row", "col"), None), P()),
        check_vma=False,
    )
```

```python
import functools

import jax
import jax.numpy as jnp
from jax import lax
from jax.experimental import pallas as pl
from jax.experimental.pallas import tpu as pltpu
from jax.sharding import PartitionSpec as P

STRIPS = 2
HEAVY = 20_000_000_000
VMEM_LIMIT = 48 * 1024 * 1024


def ring_of(count, width):
    height = count // width
    if count % width or width % 2 or height < 2:
        return list(range(count))
    walk = [(0, x) for x in range(width)]
    for turn, x in enumerate(reversed(range(width))):
        down = range(1, height) if turn % 2 == 0 else range(height - 1, 0, -1)
        walk += [(z, x) for z in down]
    return [z * width + x for z, x in walk]


def ring_slots(count):
    return [0] + [away for step in range(1, count // 2) for away in (count - step, step)] + [count // 2]


def pick(index, table):
    value = jnp.int32(table[0])
    for at in range(1, len(table)):
        value = jnp.where(index == at, jnp.int32(table[at]), value)
    return value


def position(spot):
    column = lax.axis_index("col")
    return pick(lax.axis_index("row"), spot), lax.div(column, jnp.int32(2)), lax.rem(column, jnp.int32(2))


def vmem_call(name, kernel, out_shapes, args, scratch=(), hbm=0, hbm_out=False, after=(), aliases=None, flops=0, moved=0):
    vmem = pl.BlockSpec(memory_space=pltpu.VMEM)
    anywhere = pl.BlockSpec(memory_space=pl.ANY)
    far = pl.BlockSpec(memory_space=pltpu.HBM)
    specs = [far] * hbm + [vmem] * (len(args) - hbm) + [anywhere] * len(after)
    count = len(args)

    def inner(*refs):
        kernel(*refs[:count], *refs[count + len(after) :])

    return pl.pallas_call(
        inner,
        out_shape=out_shapes,
        in_specs=specs,
        out_specs=jax.tree.map(lambda _: far if hbm_out else vmem, out_shapes),
        scratch_shapes=list(scratch),
        input_output_aliases=aliases or {},
        name=name,
        compiler_params=pltpu.CompilerParams(vmem_limit_bytes=VMEM_LIMIT),
        cost_estimate=pl.CostEstimate(flops=flops, bytes_accessed=moved, transcendentals=0),
    )(*args, *after)


def place_tiles(spot, groups, vals, tile_rows, tile_cols, tile_count, feats):
    slots, side = vals.shape[2], vals.shape[-1]
    count = len(spot)

    def kernel(row_hbm, col_hbm, live_hbm, vals_hbm, feats_hbm, out_ref, feats_ref, row_ref, col_ref, live_ref, held, sems):
        sources = (row_hbm, col_hbm, live_hbm, vals_hbm.at[0, 0], feats_hbm)
        targets = (row_ref, col_ref, live_ref, held, feats_ref)
        copies = [pltpu.make_async_copy(a, b, sems.at[k]) for k, (a, b) in enumerate(zip(sources, targets))]
        for copy in copies:
            copy.start()
        me, group, core = position(spot)
        out_ref[...] = jnp.zeros_like(out_ref)
        for copy in copies:
            copy.wait()

        def put(slot, carry):
            row = row_ref[0, 0, slot]
            other = lax.rem(row, 2) ^ core
            along = lax.rem(lax.div(row, 2) + groups - group, groups)
            top = pl.multiple_of((other * groups + along) * side, side)
            away = lax.rem(pick(col_ref[0, 0, slot], spot) + count - me, count)
            col = jnp.where(away < count // 2, 2 * away, 2 * (count - away) - 1)
            left = pl.multiple_of(col * side, side)
            out_ref[pl.ds(top, side), pl.ds(left, side)] = held[slot]
            return carry

        lax.fori_loop(0, live_ref[0, 0], put, 0)

    shapes = (
        jax.ShapeDtypeStruct((2 * groups * side, count * side), vals.dtype),
        jax.ShapeDtypeStruct(feats.shape, feats.dtype),
    )
    args = (tile_rows, tile_cols, tile_count, vals, feats)
    scratch = [pltpu.SMEM(a.shape, a.dtype) for a in args[:3]]
    scratch += [pltpu.VMEM((slots, side, side), vals.dtype), pltpu.SemaphoreType.DMA((5,))]
    return vmem_call("place_tiles", kernel, shapes, args, scratch=scratch, hbm=5, moved=4 * vals.size)


def gate(values, after, flops=0):
    def kernel(*refs):
        del refs

    shapes = [jax.ShapeDtypeStruct(v.shape, v.dtype) for v in values]
    return vmem_call("gate", kernel, shapes, values, after=after, flops=flops, aliases={k: k for k in range(len(values))})


def aggregate(adjacency, pieces, ends, part, parts, after):
    rows, depth = adjacency.shape
    height, width = pieces[0].shape
    half, strip = rows // 2, width // parts
    columns = slice(part * strip, (part + 1) * strip)

    def kernel(*refs):
        adj_ref = refs[0]
        piece_refs = refs[1 : 1 + len(pieces)]
        right_ref, left_ref, near_ref, far_ref, held = refs[1 + len(pieces) :]
        for place, piece_ref in enumerate(piece_refs):
            held[place * height : (place + 1) * height] = piece_ref[:, columns]
        held[depth - height :] = jnp.concatenate([right_ref[...], left_ref[...]], axis=1)[:, columns]
        far_ref[...] = jnp.dot(adj_ref[half:], held[...], preferred_element_type=jnp.float32).astype(jnp.bfloat16)
        near_ref[...] = jnp.dot(adj_ref[:half], held[...], preferred_element_type=jnp.float32)

    shapes = (
        jax.ShapeDtypeStruct((half, strip), jnp.float32),
        jax.ShapeDtypeStruct((half, strip), jnp.bfloat16),
    )
    return vmem_call(
        "aggregate",
        kernel,
        shapes,
        (adjacency, *pieces, *ends),
        scratch=[pltpu.VMEM((depth, strip), jnp.bfloat16)],
        after=after,
        flops=2 * rows * depth * strip,
        moved=2 * (rows * depth + depth * strip + rows * strip),
    )


def dense(spot, held, arrived, weight, cotangents):
    chunks = len(held)
    rows, width = held[0].shape
    depth, cols = weight.shape
    groups = len(cotangents)
    side = rows // groups
    part = depth // groups
    quarter = part // 2

    def kernel(*refs):
        refs = list(refs)
        _, group, core = position(spot)
        held_refs = [refs.pop(0) for _ in range(chunks)]
        arrived_refs = [[refs.pop(0) for _ in range(chunks)] for _ in range(groups - 1)]
        weight_ref = refs.pop(0)
        cot_refs = [refs.pop(0) for _ in range(groups)]
        act_ref, near_ref, far_ref = refs[:3]
        back_ref = refs[3]
        agg = refs[-2]
        grad = refs[-1]
        for h in range(chunks):
            for g in range(groups):
                total = held_refs[h][g * side : (g + 1) * side].astype(jnp.float32)
                for s in range(1, groups):
                    at = (g + s) % groups
                    total = total + arrived_refs[s - 1][h][at * side : (at + 1) * side].astype(jnp.float32)
                agg[g * side : (g + 1) * side, h * width : (h + 1) * width] = total.astype(jnp.bfloat16)
        for g in range(groups):
            value = jnp.dot(agg[g * side : (g + 1) * side], weight_ref[...], preferred_element_type=jnp.float32)
            gate = jax.nn.sigmoid(value)
            if g == 0:
                act_ref[...] = (value * gate).astype(jnp.bfloat16)
            slope = gate * (1.0 + value * (1.0 - gate))
            cot = cot_refs[(groups - g) % groups][...].astype(jnp.float32)
            grad[g * side : (g + 1) * side] = (cot * slope).astype(jnp.bfloat16)
        back_ref[...] = lax.dot_general(
            grad[...], weight_ref[...], (((1,), (1,)), ((), ())), preferred_element_type=jnp.float32
        ).astype(jnp.bfloat16)
        first = group * part
        near_at = pl.multiple_of(first + core * quarter, 128)
        far_at = pl.multiple_of(first + (1 - core) * quarter, 128)
        far_ref[...] = lax.dot_general(
            agg[:, pl.ds(far_at, quarter)], grad[...], (((0,), (0,)), ((), ())), preferred_element_type=jnp.float32
        ).astype(jnp.bfloat16)
        near_ref[...] = lax.dot_general(
            agg[:, pl.ds(near_at, quarter)], grad[...], (((0,), (0,)), ((), ())), preferred_element_type=jnp.float32
        )

    shapes = [
        jax.ShapeDtypeStruct((side, cols), jnp.bfloat16),
        jax.ShapeDtypeStruct((quarter, cols), jnp.float32),
        jax.ShapeDtypeStruct((quarter, cols), jnp.bfloat16),
        jax.ShapeDtypeStruct((rows, depth), jnp.bfloat16),
    ]
    outs = vmem_call(
        "dense",
        kernel,
        shapes,
        (*held, *[a for step in arrived for a in step], weight, *cotangents),
        scratch=[pltpu.VMEM((rows, depth), jnp.bfloat16), pltpu.VMEM((rows, cols), jnp.bfloat16)],
        flops=2 * rows * cols * (2 * depth + part),
        moved=2 * (depth * cols + 6 * rows * depth),
    )
    return outs


def back_blocks(adjacency, near, far, count):
    rows, depth = adjacency.shape
    half, width = near.shape
    height = depth // count

    def kernel(adj_ref, near_ref, far_ref, *out_refs):
        held = out_refs[-1]
        held[:half] = near_ref[...]
        held[half:] = far_ref[...]
        for place in reversed(range(count)):
            block = lax.dot_general(
                adj_ref[:, place * height : (place + 1) * height],
                held[...],
                (((0,), (0,)), ((), ())),
                preferred_element_type=jnp.float32,
            ).astype(jnp.bfloat16)
            if place == count - 1:
                out_refs[place][...] = block[:, : width // 2]
                out_refs[place + 1][...] = block[:, width // 2 :]
            else:
                out_refs[place][...] = block

    shapes = [jax.ShapeDtypeStruct((height, width), jnp.bfloat16)] * (count - 1)
    shapes += [jax.ShapeDtypeStruct((height, width // 2), jnp.bfloat16)] * 2
    return vmem_call(
        "back_blocks",
        kernel,
        shapes,
        (adjacency, near, far),
        scratch=[pltpu.VMEM((rows, width), jnp.bfloat16)],
        flops=2 * rows * depth * width,
        moved=2 * (rows * depth + depth * width + rows * width),
    )


def weight_blocks(spot, near, arrived):
    count = len(spot)
    rows, cols = near.shape
    share, middle = rows // count, cols // 2

    def kernel(near_ref, arrived_ref, *refs):
        total = refs[-1]
        me, _, _ = position(spot)
        total[...] = near_ref[...] + arrived_ref[...].astype(jnp.float32)
        for place, away in enumerate(ring_slots(count)):
            at = pl.multiple_of(lax.rem(me + away, count) * share, share)
            block = total[pl.ds(at, share)].astype(jnp.bfloat16)
            if place == count - 1:
                refs[place][...] = block[:, :middle]
                refs[place + 1][...] = block[:, middle:]
            else:
                refs[place][...] = block

    shapes = [jax.ShapeDtypeStruct((share, cols), jnp.bfloat16)] * (count - 1)
    shapes += [jax.ShapeDtypeStruct((share, middle), jnp.bfloat16)] * 2
    scratch = [pltpu.VMEM(near.shape, jnp.float32)]
    return vmem_call("weight_blocks", kernel, shapes, (near, arrived), scratch=scratch, flops=near.size, moved=8 * near.size)


def add_round(pairs, finals, carried=(), after=(), flops=0):
    args = [a for group in pairs + finals for a in group] + list(carried)

    def kernel(*refs):
        ins, outs = list(refs[: len(args)]), list(refs[len(args) :])
        for _ in pairs:
            right, left, first, second = (ins.pop(0) for _ in range(4))
            width, part = right.shape[1], first.shape[1]
            out_right, out_left = outs.pop(0), outs.pop(0)
            out_right[:, :part] = right[:, :part] + first[...]
            out_left[:, width - part :] = left[:, width - part :] + second[...]
            if part < width:
                out_right[:, part:] = right[:, part:]
                out_left[:, : width - part] = left[:, : width - part]
        for _ in finals:
            own, first, second = (ins.pop(0)[...].astype(jnp.float32) for _ in range(3))
            outs.pop(0)[...] = (own + first + second).astype(jnp.bfloat16)
        for _ in carried:
            outs.pop(0)[...] = ins.pop(0)[...]

    shapes = [jax.ShapeDtypeStruct(g[0].shape, jnp.bfloat16) for g in pairs for _ in range(2)]
    shapes += [jax.ShapeDtypeStruct(g[0].shape, jnp.bfloat16) for g in finals]
    shapes += [jax.ShapeDtypeStruct(a.shape, jnp.bfloat16) for a in carried]
    moved = sum(4 * a.size for a in args)
    outs = vmem_call("add_round", kernel, shapes, args, after=after, flops=flops, moved=moved)
    return [tuple(outs[2 * k : 2 * k + 2]) for k in range(len(pairs))], outs[2 * len(pairs) :]


def stack_blocks(blocks, ends, after):
    height, width = (blocks or ends)[0].shape
    if not blocks:
        width *= 2

    def kernel(*refs):
        out_ref = refs[-1]
        for place in range(len(blocks)):
            out_ref[place * height : (place + 1) * height] = refs[place][...]
        for side in range(len(ends)):
            half = width // 2
            out_ref[len(blocks) * height :, side * half : (side + 1) * half] = refs[len(blocks) + side][...]

    total = len(blocks) + len(ends) // 2
    shape = jax.ShapeDtypeStruct((total * height, width), jnp.bfloat16)
    return vmem_call("stack_blocks", kernel, shape, (*blocks, *ends), after=after, moved=4 * total * height * width)


def join_weight(spot, groups, shape, stacks, begun=None):
    count = len(spot)
    quarter = shape[0] // (2 * groups)
    share = quarter // count
    total = sum(len(s[1]) for s in stacks)

    def kernel(*refs):
        stack_refs = refs[0 if begun is None else 1 :]
        out_ref, wide, sems = refs[-3:]
        me, group, core = position(spot)
        copies = []
        for ref, (_, aways, steps, other) in zip(stack_refs, stacks):
            back = lax.rem(group + groups - steps, groups)
            base = (back * 2 + (1 - core if other else core)) * quarter
            for place, away in enumerate(aways):
                slot = len(copies)
                wide[slot] = ref[place * share : (place + 1) * share].astype(jnp.float32)
                at = pl.multiple_of(base + lax.rem(me + away, count) * share, share)
                copies.append(pltpu.make_async_copy(wide.at[slot], out_ref.at[pl.ds(at, share)], sems.at[slot]))
                copies[-1].start()
        for copy in copies:
            copy.wait()

    out = jax.ShapeDtypeStruct(shape, jnp.float32)
    scratch = [pltpu.VMEM((total, share, shape[1]), jnp.float32), pltpu.SemaphoreType.DMA((total,))]
    args = [s[0] for s in stacks]
    moved = 6 * total * share * shape[1]
    flops = HEAVY
    if begun is None:
        return vmem_call("join_weight", kernel, out, args, scratch=scratch, hbm_out=True, flops=flops, moved=moved)
    return vmem_call("join_weight", kernel, out, [begun, *args], scratch=scratch, hbm=1, hbm_out=True, aliases={0: 0}, flops=flops, moved=moved)


def body(width, feats, weight, tile_vals, tile_rows, tile_cols, tile_count, grad_out):
    count = lax.axis_size("row")
    columns = lax.axis_size("col")
    groups = columns // 2
    rounds = count // 2
    ring = ring_of(count, width)
    spot = [0] * count
    for place, row in enumerate(ring):
        spot[row] = place

    to_right = [(ring[k], ring[(k + 1) % count]) for k in range(count)]
    to_left = [(ring[k], ring[(k - 1) % count]) for k in range(count)]
    swap = [(k, k ^ 1) for k in range(columns)]

    def go(label, right, left):
        with jax.named_scope(label):
            return lax.ppermute(right, "row", to_right), lax.ppermute(left, "row", to_left)

    def go_halves(label, right, left):
        middle = right.shape[1] // 2
        return go(label, right[:, :middle], left[:, middle:])

    def swap_core(label, value):
        with jax.named_scope(label):
            return lax.ppermute(value, "col", swap)

    def from_group(label, value, steps):
        with jax.named_scope(label):
            return lax.ppermute(value, "col", [(k, (k + 2 * steps) % columns) for k in range(columns)])

    adjacency, near_feats = place_tiles(spot, groups, tile_vals, tile_rows, tile_cols, tile_count, feats)
    cotangents = [grad_out] + [from_group("cotangent_y", grad_out, s) for s in range(1, groups)]
    pieces = [near_feats]
    moving = (feats, feats)
    for step in range(1, rounds + 1):
        if step == 2:
            moving = gate(moving, [adjacency])
        if step > 1:
            pieces += moving
        send = go if step < rounds else go_halves
        moving = send(f"feature_ring_{step}", *moving)

    held = []
    arrived = [[] for _ in range(groups - 1)]
    for h in range(STRIPS):
        near, far = aggregate(adjacency, pieces, moving, h, STRIPS, cotangents[1:])
        total = (near + swap_core(f"sum_core_{h}", far).astype(jnp.float32)).astype(jnp.bfloat16)
        held.append(total)
        for s in range(1, groups):
            arrived[s - 1].append(from_group(f"sum_y_{h}", total, s))

    activated, near_weight, far_weight, back = dense(spot, held, arrived, weight, cotangents)

    slots = ring_slots(count)
    cuts = (0, 3, count - 3, count - 1, count)
    stacks = []

    def spread_part(part, after=()):
        first, last = cuts[part], cuts[part + 1]
        stack = stack_blocks(pieces[first:last], weight_moving if last == count else (), after)
        found = []
        for s in range(groups):
            value = stack if s == 0 else from_group(f"weight_y_{part}", stack, s)
            found.append((value, slots[first:last], s, False))
            found.append((swap_core(f"weight_last_{part}", value), slots[first:last], s, True))
        stacks.append(found)

    far_weight = swap_core("weight_core", far_weight)
    far_back = swap_core("back_core", back)
    terms = weight_blocks(spot, near_weight, far_weight)
    blocks = back_blocks(adjacency, back, far_back, count)
    pieces = []
    moving = weight_moving = None
    for turn in range(2 * rounds):
        j, odd = divmod(turn, 2)
        pairs, finals, carried, after = [], [], [], []
        if 0 < turn < rounds:
            step = 2 * (rounds - turn)
            pairs.append((terms[step], terms[step - 1], *weight_moving))
        elif turn == rounds:
            finals.append((terms[0], *weight_moving))
        elif turn > rounds:
            carried = weight_moving
            if turn == 2 * rounds - 1:
                after = [found[0] for found in stacks[0]]
        if j > 0 and not odd:
            step = 2 * (rounds - j)
            pairs.append((blocks[step], blocks[step - 1], *moving))
        if turn > 0:
            sums, ends = add_round(pairs, finals, carried, after, HEAVY if odd else 0)
        label = f"weight_ring_{turn}"
        if turn == 0:
            weight_moving = go(label, terms[count - 1], terms[count])
        elif turn < rounds:
            weight_moving = go(label, *sums[0])
        elif turn == rounds:
            pieces.append(ends[0])
            weight_moving = go(label, ends[0], ends[0])
        else:
            pieces += weight_moving
            send = go if turn < 2 * rounds - 1 else go_halves
            weight_moving = send(label, *ends)
            if len(pieces) in cuts:
                spread_part(cuts.index(len(pieces)) - 1)
        label = f"back_ring_{j}"
        if turn == 0:
            moving = go(label, blocks[count - 1], blocks[count])
        elif not odd:
            moving = go(label, *sums[-1])
    _, (grad_feats,) = add_round([], [(blocks[0], *moving)])

    spread_part(3, [*moving, *(found[0] for found in stacks[1])])
    grad_weight = None
    for part in range(4):
        grad_weight = join_weight(spot, groups, weight.shape, stacks[part], grad_weight)
    return (activated, grad_feats, grad_weight)


def solution(mesh):
    spread = {d.coords[0] for d in mesh.devices.flat if hasattr(d, "coords")}
    placed = (
        P(("row", "col"), None),
        P(),
        P("row", "col", None, None, None),
        P("row", "col", None),
        P("row", "col", None),
        P("row", "col"),
        P(("row", "col"), None),
    )
    return jax.shard_map(
        functools.partial(body, max(1, len(spread))),
        mesh=mesh,
        in_specs=placed,
        out_specs=(P(("row", "col"), None), P(("row", "col"), None), P()),
        check_vma=False,
    )
```

```python
import functools

import jax
import jax.numpy as jnp
from jax import lax
from jax.experimental import pallas as pl
from jax.experimental.pallas import tpu as pltpu
from jax.sharding import PartitionSpec as P

LONG = 20_000_000_000
VMEM_LIMIT = 48 * 1024 * 1024


def ring_of(count, width):
    height = count // width
    if count % width or width % 2 or height < 2:
        return list(range(count))
    walk = [(0, x) for x in range(width)]
    for turn, x in enumerate(reversed(range(width))):
        down = range(1, height) if turn % 2 == 0 else range(height - 1, 0, -1)
        walk += [(z, x) for z in down]
    return [z * width + x for z, x in walk]


def ring_slots(count):
    return [0] + [away for step in range(1, count // 2) for away in (count - step, step)] + [count // 2]


def pick(index, table):
    value = jnp.int32(table[0])
    for at in range(1, len(table)):
        value = jnp.where(index == at, jnp.int32(table[at]), value)
    return value


def position(spot):
    column = lax.axis_index("col")
    return pick(lax.axis_index("row"), spot), lax.div(column, jnp.int32(2)), lax.rem(column, jnp.int32(2))


def vmem_call(name, kernel, out_shapes, args, scratch=(), hbm=0, hbm_out=False, after=(), aliases=None, flops=0, moved=0):
    vmem = pl.BlockSpec(memory_space=pltpu.VMEM)
    anywhere = pl.BlockSpec(memory_space=pl.ANY)
    far = pl.BlockSpec(memory_space=pltpu.HBM)
    specs = [far] * hbm + [vmem] * (len(args) - hbm) + [anywhere] * len(after)
    count = len(args)

    def inner(*refs):
        kernel(*refs[:count], *refs[count + len(after) :])

    return pl.pallas_call(
        inner,
        out_shape=out_shapes,
        in_specs=specs,
        out_specs=jax.tree.map(lambda _: far if hbm_out else vmem, out_shapes),
        scratch_shapes=list(scratch),
        input_output_aliases=aliases or {},
        name=name,
        compiler_params=pltpu.CompilerParams(vmem_limit_bytes=VMEM_LIMIT),
        cost_estimate=pl.CostEstimate(flops=flops, bytes_accessed=moved, transcendentals=0),
    )(*args, *after)


def place_tiles(spot, groups, vals, tile_rows, tile_cols, tile_count, feats):
    slots, side = vals.shape[2], vals.shape[-1]
    count = len(spot)

    def kernel(row_hbm, col_hbm, live_hbm, vals_hbm, feats_hbm, out_ref, feats_ref, row_ref, col_ref, live_ref, held, sems):
        sources = (row_hbm, col_hbm, live_hbm, vals_hbm.at[0, 0], feats_hbm)
        targets = (row_ref, col_ref, live_ref, held, feats_ref)
        copies = [pltpu.make_async_copy(a, b, sems.at[k]) for k, (a, b) in enumerate(zip(sources, targets))]
        for copy in copies:
            copy.start()
        me, group, core = position(spot)
        out_ref[...] = jnp.zeros_like(out_ref)
        for copy in copies:
            copy.wait()

        def put(slot, carry):
            row = row_ref[0, 0, slot]
            other = lax.rem(row, 2) ^ core
            along = lax.rem(lax.div(row, 2) + groups - group, groups)
            top = pl.multiple_of((other * groups + along) * side, side)
            away = lax.rem(pick(col_ref[0, 0, slot], spot) + count - me, count)
            col = jnp.where(away < count // 2, 2 * away, 2 * (count - away) - 1)
            left = pl.multiple_of(col * side, side)
            out_ref[pl.ds(top, side), pl.ds(left, side)] = held[slot]
            return carry

        lax.fori_loop(0, live_ref[0, 0], put, 0)

    shapes = (
        jax.ShapeDtypeStruct((2 * groups * side, count * side), vals.dtype),
        jax.ShapeDtypeStruct(feats.shape, feats.dtype),
    )
    args = (tile_rows, tile_cols, tile_count, vals, feats)
    scratch = [pltpu.SMEM(a.shape, a.dtype) for a in args[:3]]
    scratch += [pltpu.VMEM((slots, side, side), vals.dtype), pltpu.SemaphoreType.DMA((5,))]
    return vmem_call("place_tiles", kernel, shapes, args, scratch=scratch, hbm=5, moved=4 * vals.size)


def gate(values, after):
    def kernel(*refs):
        del refs

    shapes = [jax.ShapeDtypeStruct(v.shape, v.dtype) for v in values]
    return vmem_call("gate", kernel, shapes, values, after=after, aliases={k: k for k in range(len(values))})


def aggregate(adjacency, pieces):
    rows, depth = adjacency.shape
    height, width = pieces[0].shape
    known = len(pieces) * height

    def kernel(*refs):
        adj_ref, out_ref, held = refs[0], refs[-2], refs[-1]
        for place in range(len(pieces)):
            held[place * height : (place + 1) * height] = refs[1 + place][...]
        out_ref[...] = jnp.dot(adj_ref[:, :known], held[...], preferred_element_type=jnp.float32)

    return vmem_call(
        "aggregate",
        kernel,
        jax.ShapeDtypeStruct((rows, width), jnp.float32),
        (adjacency, *pieces),
        scratch=[pltpu.VMEM((known, width), jnp.bfloat16)],
        flops=2 * rows * known * width,
        moved=2 * (rows * depth + known * width + 2 * rows * width),
    )


def aggregate_last(adjacency, known, ends, side, after):
    rows, depth = adjacency.shape
    height, middle = ends[0].shape
    half = rows // 2

    def kernel(adj_ref, known_ref, right_ref, left_ref, near_own, near_rest, far_own, far_rest):
        last = slice(depth - height, depth)
        for first, count, out_ref in (
            (half + side, half - side, far_rest),
            (half, side, far_own),
            (side, half - side, near_rest),
            (0, side, near_own),
        ):
            here = slice(first, first + count)
            for columns, end_ref in ((slice(0, middle), right_ref), (slice(middle, 2 * middle), left_ref)):
                term = jnp.dot(adj_ref[here, last], end_ref[...], preferred_element_type=jnp.float32)
                out_ref[:, columns] = (known_ref[here, columns] + term).astype(out_ref.dtype)

    shapes = [jax.ShapeDtypeStruct((n, 2 * middle), t) for t in (jnp.float32, jnp.bfloat16) for n in (side, half - side)]
    flops = 4 * rows * height * middle
    return vmem_call(
        "aggregate_last", kernel, shapes, (adjacency, known, *ends), after=after, flops=flops, moved=16 * rows * middle
    )


def slopes(value, cotangent):
    gate = jax.nn.sigmoid(value)
    slope = gate * (1.0 + value * (1.0 - gate))
    return gate, (cotangent.astype(jnp.float32) * slope).astype(jnp.bfloat16)


def times_transposed(left, right):
    return lax.dot_general(left, right, (((1,), (1,)), ((), ())), preferred_element_type=jnp.float32).astype(jnp.bfloat16)


def dense_own(held, arrived, weight, cotangent):
    side, depth = held.shape
    cols = weight.shape[1]

    def kernel(*refs):
        held_ref, weight_ref, cot_ref = refs[0], refs[-6], refs[-5]
        act_ref, agg_ref, grad_ref, back_ref = refs[-4:]
        total = held_ref[...].astype(jnp.float32)
        for ref in refs[1 : 1 + len(arrived)]:
            total = total + ref[...].astype(jnp.float32)
        agg_ref[...] = total.astype(jnp.bfloat16)
        value = jnp.dot(agg_ref[...], weight_ref[...], preferred_element_type=jnp.float32)
        gate, grad = slopes(value, cot_ref[...])
        act_ref[...] = (value * gate).astype(jnp.bfloat16)
        grad_ref[...] = grad
        back_ref[...] = times_transposed(grad, weight_ref[...])

    shapes = [jax.ShapeDtypeStruct((side, n), jnp.bfloat16) for n in (cols, depth, cols, depth)]
    return vmem_call(
        "dense_own",
        kernel,
        shapes,
        (held, *arrived, weight, cotangent),
        flops=4 * side * cols * depth,
        moved=2 * (depth * cols + 6 * side * depth),
    )


def dense_rest(spot, held, arrived, weight, cotangents, agg_own, grad_own):
    rows, depth = held.shape
    side = agg_own.shape[0]
    cols = weight.shape[1]
    part = depth // (rows // side + 1)
    quarter = part // 2

    def kernel(*refs):
        held_ref, weight_ref = refs[0], refs[1 + len(arrived)]
        cot_refs = refs[2 + len(arrived) : 2 + len(arrived) + len(cotangents)]
        agg_ref, grad_ref, near_ref, far_ref, back_ref, agg, grad = refs[-7:]
        _, group, core = position(spot)
        total = held_ref[...].astype(jnp.float32)
        for ref in refs[1 : 1 + len(arrived)]:
            total = total + ref[...].astype(jnp.float32)
        agg[:side] = agg_ref[...]
        grad[:side] = grad_ref[...]
        agg[side:] = total.astype(jnp.bfloat16)
        value = jnp.dot(agg[side:], weight_ref[...], preferred_element_type=jnp.float32)
        for g, cot_ref in enumerate(cot_refs):
            _, piece = slopes(value[g * side : (g + 1) * side], cot_ref[...])
            grad[(g + 1) * side : (g + 2) * side] = piece
        first = group * part
        far_at = pl.multiple_of(first + (1 - core) * quarter, 128)
        near_at = pl.multiple_of(first + core * quarter, 128)
        far_ref[...] = lax.dot_general(
            agg[:, pl.ds(far_at, quarter)], grad[...], (((0,), (0,)), ((), ())), preferred_element_type=jnp.float32
        ).astype(jnp.bfloat16)
        near_ref[...] = lax.dot_general(
            agg[:, pl.ds(near_at, quarter)], grad[...], (((0,), (0,)), ((), ())), preferred_element_type=jnp.float32
        )
        back_ref[...] = times_transposed(grad[side:], weight_ref[...])

    shapes = [
        jax.ShapeDtypeStruct((quarter, cols), jnp.float32),
        jax.ShapeDtypeStruct((quarter, cols), jnp.bfloat16),
        jax.ShapeDtypeStruct((rows, depth), jnp.bfloat16),
    ]
    return vmem_call(
        "dense_rest",
        kernel,
        shapes,
        (held, *arrived, weight, *cotangents, agg_own, grad_own),
        scratch=[pltpu.VMEM((side + rows, depth), jnp.bfloat16), pltpu.VMEM((side + rows, cols), jnp.bfloat16)],
        flops=4 * rows * cols * depth + 2 * (rows + side) * part * cols,
        moved=2 * (depth * cols + 6 * rows * depth),
    )


def back_blocks(adjacency, parts, count):
    rows, depth = adjacency.shape
    width = parts[0].shape[1]
    height = depth // count

    def kernel(adj_ref, *refs):
        out_refs, held = refs[len(parts) :], refs[-1]
        first = 0
        for ref in refs[: len(parts)]:
            held[first : first + ref.shape[0]] = ref[...]
            first += ref.shape[0]
        for place in reversed(range(count)):
            block = lax.dot_general(
                adj_ref[:, place * height : (place + 1) * height],
                held[...],
                (((0,), (0,)), ((), ())),
                preferred_element_type=jnp.float32,
            ).astype(jnp.bfloat16)
            if place == count - 1:
                out_refs[place][...] = block[:, : width // 2]
                out_refs[place + 1][...] = block[:, width // 2 :]
            else:
                out_refs[place][...] = block

    shapes = [jax.ShapeDtypeStruct((height, width), jnp.bfloat16)] * (count - 1)
    shapes += [jax.ShapeDtypeStruct((height, width // 2), jnp.bfloat16)] * 2
    return vmem_call(
        "back_blocks",
        kernel,
        shapes,
        (adjacency, *parts),
        scratch=[pltpu.VMEM((rows, width), jnp.bfloat16)],
        flops=2 * rows * depth * width,
        moved=2 * (rows * depth + depth * width + rows * width),
    )


def weight_blocks(spot, near, arrived):
    count = len(spot)
    rows, cols = near.shape
    share, middle = rows // count, cols // 2

    def kernel(near_ref, arrived_ref, *refs):
        total = refs[-1]
        me, _, _ = position(spot)
        total[...] = near_ref[...] + arrived_ref[...].astype(jnp.float32)
        for place, away in enumerate(ring_slots(count)):
            at = pl.multiple_of(lax.rem(me + away, count) * share, share)
            block = total[pl.ds(at, share)].astype(jnp.bfloat16)
            if place == count - 1:
                refs[place][...] = block[:, :middle]
                refs[place + 1][...] = block[:, middle:]
            else:
                refs[place][...] = block

    shapes = [jax.ShapeDtypeStruct((share, cols), jnp.bfloat16)] * (count - 1)
    shapes += [jax.ShapeDtypeStruct((share, middle), jnp.bfloat16)] * 2
    scratch = [pltpu.VMEM(near.shape, jnp.float32)]
    return vmem_call("weight_blocks", kernel, shapes, (near, arrived), scratch=scratch, flops=near.size, moved=8 * near.size)


def add_round(sums, carried, after, flops):
    args = [a for entry in sums for a in entry[:2]] + list(carried)

    def kernel(*refs):
        ins, outs = list(refs[: len(args)]), list(refs[len(args) :])
        for _, _, side in sums:
            block, arrived, out = ins.pop(0), ins.pop(0), outs.pop(0)
            width, part = block.shape[1], arrived.shape[1]
            first = (width - part) * side
            if part < width:
                out[...] = block[...]
            out[:, first : first + part] = block[:, first : first + part] + arrived[...]
        for _ in carried:
            outs.pop(0)[...] = ins.pop(0)[...]

    shapes = [jax.ShapeDtypeStruct(entry[0].shape, jnp.bfloat16) for entry in sums]
    shapes += [jax.ShapeDtypeStruct(a.shape, jnp.bfloat16) for a in carried]
    moved = sum(4 * a.size for a in args)
    return vmem_call("add_round", kernel, shapes, args, after=after, flops=flops, moved=moved)


def end_sum(own, first, second, flops):
    def kernel(own_ref, first_ref, second_ref, out_ref):
        total = own_ref[...].astype(jnp.float32) + first_ref[...].astype(jnp.float32) + second_ref[...].astype(jnp.float32)
        out_ref[...] = total.astype(jnp.bfloat16)

    shape = jax.ShapeDtypeStruct(own.shape, jnp.bfloat16)
    return vmem_call("end_sum", kernel, shape, (own, first, second), flops=flops, moved=8 * own.size)


def stack_blocks(blocks, ends=(), after=(), flops=0):
    height, width = (blocks or ends)[0].shape
    if not blocks:
        width *= 2

    def kernel(*refs):
        out_ref = refs[-1]
        for place in range(len(blocks)):
            out_ref[place * height : (place + 1) * height] = refs[place][...]
        for side in range(len(ends)):
            half = width // 2
            out_ref[len(blocks) * height :, side * half : (side + 1) * half] = refs[len(blocks) + side][...]

    total = len(blocks) + len(ends) // 2
    shape = jax.ShapeDtypeStruct((total * height, width), jnp.bfloat16)
    return vmem_call("stack_blocks", kernel, shape, (*blocks, *ends), flops=flops, after=after, moved=4 * total * height * width)


def join_weight(spot, groups, shape, stacks, begun, flops):
    count = len(spot)
    quarter = shape[0] // (2 * groups)
    share = quarter // count
    total = sum(len(s[1]) for s in stacks)
    args = [s[0] for s in stacks]
    out = jax.ShapeDtypeStruct(shape, jnp.float32)
    scratch = [pltpu.VMEM((total, share, shape[1]), jnp.float32), pltpu.SemaphoreType.DMA((total,))]

    def kernel(*refs):
        refs = refs[0 if begun is None else 1 :]
        out_ref, wide, sems = refs[-3:]
        me, group, core = position(spot)
        copies = []
        for ref, (_, aways, steps, other) in zip(refs, stacks):
            back = lax.rem(group + groups - steps, groups)
            base = (back * 2 + (1 - core if other else core)) * quarter
            for place, away in enumerate(aways):
                slot = len(copies)
                wide[slot] = ref[place * share : (place + 1) * share].astype(jnp.float32)
                at = pl.multiple_of(base + lax.rem(me + away, count) * share, share)
                copies.append(pltpu.make_async_copy(wide.at[slot], out_ref.at[pl.ds(at, share)], sems.at[slot]))
                copies[-1].start()
        for copy in copies:
            copy.wait()

    hbm = 0 if begun is None else 1
    return vmem_call(
        "join_weight",
        kernel,
        out,
        [begun] * hbm + args,
        scratch=scratch,
        hbm=hbm,
        hbm_out=True,
        aliases={0: 0} if hbm else None,
        flops=flops,
        moved=6 * total * share * shape[1],
    )


def body(width, feats, weight, tile_vals, tile_rows, tile_cols, tile_count, grad_out):
    count = lax.axis_size("row")
    columns = lax.axis_size("col")
    groups = columns // 2
    rounds = count // 2
    ring = ring_of(count, width)
    spot = [0] * count
    for place, row in enumerate(ring):
        spot[row] = place

    to_right = [(ring[k], ring[(k + 1) % count]) for k in range(count)]
    to_left = [(ring[k], ring[(k - 1) % count]) for k in range(count)]
    swap = [(k, k ^ 1) for k in range(columns)]

    def go(label, right, left):
        with jax.named_scope(label):
            return lax.ppermute(right, "row", to_right), lax.ppermute(left, "row", to_left)

    def go_halves(label, right, left):
        middle = right.shape[1] // 2
        return go(label, right[:, :middle], left[:, middle:])

    def swap_core(label, value):
        with jax.named_scope(label):
            return lax.ppermute(value, "col", swap)

    def from_group(label, value, steps):
        with jax.named_scope(label):
            return lax.ppermute(value, "col", [(k, (k + 2 * steps) % columns) for k in range(columns)])

    adjacency, near_feats = place_tiles(spot, groups, tile_vals, tile_rows, tile_cols, tile_count, feats)
    cotangents = [grad_out] + [from_group("cotangent_y", grad_out, s) for s in range(1, groups)]
    pieces = [near_feats]
    moving = (feats, feats)
    for step in range(1, rounds + 1):
        if step == 2:
            moving = gate(moving, [adjacency])
        if step > 1:
            pieces += moving
        send = go if step < rounds else go_halves
        moving = send(f"feature_ring_{step}", *moving)

    known = aggregate(adjacency, pieces)
    near_own, near_rest, far_own, far_rest = aggregate_last(adjacency, known, moving, feats.shape[0], cotangents[1:])
    rest = (near_rest + swap_core("sum_core_rest", far_rest).astype(jnp.float32)).astype(jnp.bfloat16)
    own = (near_own + swap_core("sum_core_own", far_own).astype(jnp.float32)).astype(jnp.bfloat16)
    side = feats.shape[0]
    parts = [own] + [rest[g * side : (g + 1) * side] for g in range(groups - 1)]
    arrived_own = [from_group(f"sum_y_own_{s}", parts[s], s) for s in range(1, groups)]
    arrived_rest = []
    for s in range(1, groups):
        sent = [parts[(s + g) % groups] for g in range(1, groups)]
        arrived_rest.append(from_group(f"sum_y_rest_{s}", jnp.concatenate(sent) if len(sent) > 1 else sent[0], s))
    activated, agg_own, grad_own, back_own = dense_own(own, arrived_own, weight, cotangents[0])
    turned = [cotangents[groups - g] for g in range(1, groups)]
    near_weight, far_weight, back_rest = dense_rest(spot, rest, arrived_rest, weight, turned, agg_own, grad_own)

    far_weight = swap_core("weight_core", far_weight)
    far_back = [swap_core("back_core_own", back_own), swap_core("back_core_rest", back_rest)]
    terms = weight_blocks(spot, near_weight, far_weight)
    blocks = back_blocks(adjacency, [back_own, back_rest, *far_back], count)
    slots = ring_slots(count)
    starts = [(2 * k * (2 * rounds - 1) + rounds - 1) // (2 * rounds - 2) for k in range(rounds)]
    pieces = []
    weight_moving = [terms[count - 1], terms[count]]
    moving = [blocks[count - 1], blocks[count]]
    early = early_from = None
    ordered = []
    for turn in range(2 * rounds):
        flops = 0 if turn % 2 else LONG
        sums = carried = back_sums = ()
        if 0 < turn < rounds:
            sums = [(terms[2 * (rounds - turn) - side], weight_moving[side], side) for side in range(2)]
        elif turn == rounds:
            weight_moving = [end_sum(terms[0], *weight_moving, flops)] * 2
            pieces.append(weight_moving[0])
        elif turn > rounds:
            carried = weight_moving
            pieces += weight_moving
        begins = turn in starts[1:]
        if begins:
            step = 2 * (rounds - starts.index(turn))
            back_sums = [(blocks[step - side], moving[side], side) for side in range(2)]
        if begins and turn < 2 * rounds - 1:
            apart = turn < rounds
            outs = list(add_round([*sums, *(() if apart else back_sums)], carried, ordered, flops))
            weight_moving = outs[-2:] if sums or carried else weight_moving
            moving = list(add_round(back_sums, (), weight_moving, 0)) if apart else outs[:2]
            ordered = moving[:1] if apart else []
        elif turn > 0 and turn != rounds:
            for side in range(2):
                mine = [*sums[side : side + 1], *back_sums[side : side + 1]]
                outs = add_round(mine, carried[side : side + 1], ordered, 0 if side else flops)
                weight_moving[side] = outs[0] if sums else outs[-1]
                if begins:
                    moving[side] = outs[1] if sums else outs[0]
            ordered = []
        send = go_halves if turn == 2 * rounds - 1 else go
        weight_moving = list(send(f"weight_ring_{turn}", *weight_moving))
        if turn in starts:
            moving = list(go(f"back_ring_{starts.index(turn)}", *moving))
        if turn == 2 * rounds - 2:
            early = stack_blocks(pieces)
            early_from = [from_group(f"weight_y_early_{s}", early, s) for s in range(1, groups)]
    grad_feats = end_sum(blocks[0], *moving, 0)

    late = stack_blocks(pieces[count - 3 :], weight_moving, early_from, LONG)
    late_from = [from_group(f"weight_y_late_{s}", late, s) for s in range(1, groups)]

    def placed(values, steps, part):
        return [
            entry
            for s, value in zip(steps, values)
            for entry in ((value, part, s, False), (swap_core("weight_last", value), part, s, True))
        ]

    along = range(1, groups)
    stacks = placed([early, *early_from], range(groups), slots[: count - 3]) + placed([late], [0], slots[count - 3 :])
    grad_weight = join_weight(spot, groups, weight.shape, stacks, None, LONG)
    grad_weight = join_weight(spot, groups, weight.shape, placed(late_from, along, slots[count - 3 :]), grad_weight, 0)
    return (activated, grad_feats, grad_weight)


def solution(mesh):
    spread = {d.coords[0] for d in mesh.devices.flat if hasattr(d, "coords")}
    placed = (
        P(("row", "col"), None),
        P(),
        P("row", "col", None, None, None),
        P("row", "col", None),
        P("row", "col", None),
        P("row", "col"),
        P(("row", "col"), None),
    )
    return jax.shard_map(
        functools.partial(body, max(1, len(spread))),
        mesh=mesh,
        in_specs=placed,
        out_specs=(P(("row", "col"), None), P(("row", "col"), None), P()),
        check_vma=False,
    )
```

```python
import functools

import jax
import jax.numpy as jnp
from jax import lax
from jax.experimental import pallas as pl
from jax.experimental.pallas import tpu as pltpu
from jax.sharding import PartitionSpec as P

LONG = 20_000_000_000
VMEM_LIMIT = 48 * 1024 * 1024


def ring_of(count, width):
    height = count // width
    if count % width or width % 2 or height < 2:
        return list(range(count))
    walk = [(0, x) for x in range(width)]
    for turn, x in enumerate(reversed(range(width))):
        down = range(1, height) if turn % 2 == 0 else range(height - 1, 0, -1)
        walk += [(z, x) for z in down]
    return [z * width + x for z, x in walk]


def ring_slots(count):
    return [0] + [away for step in range(1, count // 2) for away in (count - step, step)] + [count // 2]


def pick(index, table):
    value = jnp.int32(table[0])
    for at in range(1, len(table)):
        value = jnp.where(index == at, jnp.int32(table[at]), value)
    return value


def position(spot):
    column = lax.axis_index("col")
    return pick(lax.axis_index("row"), spot), lax.div(column, jnp.int32(2)), lax.rem(column, jnp.int32(2))


def vmem_call(name, kernel, out_shapes, args, scratch=(), hbm=0, hbm_out=False, after=(), aliases=None, flops=0, moved=0):
    vmem = pl.BlockSpec(memory_space=pltpu.VMEM)
    anywhere = pl.BlockSpec(memory_space=pl.ANY)
    far = pl.BlockSpec(memory_space=pltpu.HBM)
    specs = [far] * hbm + [vmem] * (len(args) - hbm) + [anywhere] * len(after)
    count = len(args)

    def inner(*refs):
        kernel(*refs[:count], *refs[count + len(after) :])

    return pl.pallas_call(
        inner,
        out_shape=out_shapes,
        in_specs=specs,
        out_specs=jax.tree.map(lambda _: far if hbm_out else vmem, out_shapes),
        scratch_shapes=list(scratch),
        input_output_aliases=aliases or {},
        name=name,
        compiler_params=pltpu.CompilerParams(vmem_limit_bytes=VMEM_LIMIT),
        cost_estimate=pl.CostEstimate(flops=flops, bytes_accessed=moved, transcendentals=0),
    )(*args, *after)


def place_tiles(spot, groups, vals, tile_rows, tile_cols, tile_count, feats):
    slots, side = vals.shape[2], vals.shape[-1]
    count = len(spot)

    def kernel(row_hbm, col_hbm, live_hbm, vals_hbm, feats_hbm, out_ref, feats_ref, row_ref, col_ref, live_ref, held, sems):
        sources = (row_hbm, col_hbm, live_hbm, vals_hbm.at[0, 0], feats_hbm)
        targets = (row_ref, col_ref, live_ref, held, feats_ref)
        copies = [pltpu.make_async_copy(a, b, sems.at[k]) for k, (a, b) in enumerate(zip(sources, targets))]
        for copy in copies:
            copy.start()
        me, group, core = position(spot)
        out_ref[...] = jnp.zeros_like(out_ref)
        for copy in copies:
            copy.wait()

        def put(slot, carry):
            row = row_ref[0, 0, slot]
            other = lax.rem(row, 2) ^ core
            along = lax.rem(lax.div(row, 2) + groups - group, groups)
            top = pl.multiple_of((other * groups + along) * side, side)
            away = lax.rem(pick(col_ref[0, 0, slot], spot) + count - me, count)
            col = jnp.where(away < count // 2, 2 * away, 2 * (count - away) - 1)
            left = pl.multiple_of(col * side, side)
            out_ref[pl.ds(top, side), pl.ds(left, side)] = held[slot]
            return carry

        lax.fori_loop(0, live_ref[0, 0], put, 0)

    shapes = (
        jax.ShapeDtypeStruct((2 * groups * side, count * side), vals.dtype),
        jax.ShapeDtypeStruct(feats.shape, feats.dtype),
    )
    args = (tile_rows, tile_cols, tile_count, vals, feats)
    scratch = [pltpu.SMEM(a.shape, a.dtype) for a in args[:3]]
    scratch += [pltpu.VMEM((slots, side, side), vals.dtype), pltpu.SemaphoreType.DMA((5,))]
    return vmem_call("place_tiles", kernel, shapes, args, scratch=scratch, hbm=5, moved=4 * vals.size)


def gate(values, after):
    def kernel(*refs):
        del refs

    shapes = [jax.ShapeDtypeStruct(v.shape, v.dtype) for v in values]
    return vmem_call("gate", kernel, shapes, values, after=after, aliases={k: k for k in range(len(values))})


def aggregate(adjacency, pieces):
    rows, depth = adjacency.shape
    height, width = pieces[0].shape
    known = len(pieces) * height

    def kernel(*refs):
        adj_ref, out_ref, held = refs[0], refs[-2], refs[-1]
        for place in range(len(pieces)):
            held[place * height : (place + 1) * height] = refs[1 + place][...]
        out_ref[...] = jnp.dot(adj_ref[:, :known], held[...], preferred_element_type=jnp.float32)

    return vmem_call(
        "aggregate",
        kernel,
        jax.ShapeDtypeStruct((rows, width), jnp.float32),
        (adjacency, *pieces),
        scratch=[pltpu.VMEM((known, width), jnp.bfloat16)],
        flops=2 * rows * known * width,
        moved=2 * (rows * depth + known * width + 2 * rows * width),
    )


def aggregate_last(adjacency, known, ends, side, after):
    rows, depth = adjacency.shape
    height, middle = ends[0].shape
    half = rows // 2

    def kernel(adj_ref, known_ref, right_ref, left_ref, near_own, near_rest, far_own, far_rest):
        last = slice(depth - height, depth)
        for first, count, out_ref in (
            (half + side, half - side, far_rest),
            (half, side, far_own),
            (side, half - side, near_rest),
            (0, side, near_own),
        ):
            here = slice(first, first + count)
            for columns, end_ref in ((slice(0, middle), right_ref), (slice(middle, 2 * middle), left_ref)):
                term = jnp.dot(adj_ref[here, last], end_ref[...], preferred_element_type=jnp.float32)
                out_ref[:, columns] = (known_ref[here, columns] + term).astype(out_ref.dtype)

    shapes = [jax.ShapeDtypeStruct((n, 2 * middle), t) for t in (jnp.float32, jnp.bfloat16) for n in (side, half - side)]
    flops = 4 * rows * height * middle
    return vmem_call(
        "aggregate_last", kernel, shapes, (adjacency, known, *ends), after=after, flops=flops, moved=16 * rows * middle
    )


def slopes(value, cotangent):
    gate = jax.nn.sigmoid(value)
    slope = gate * (1.0 + value * (1.0 - gate))
    return gate, (cotangent.astype(jnp.float32) * slope).astype(jnp.bfloat16)


def times_transposed(left, right):
    return lax.dot_general(left, right, (((1,), (1,)), ((), ())), preferred_element_type=jnp.float32).astype(jnp.bfloat16)


def dense_own(held, arrived, weight, cotangent):
    side, depth = held.shape
    cols = weight.shape[1]

    def kernel(*refs):
        held_ref, weight_ref, cot_ref = refs[0], refs[-6], refs[-5]
        act_ref, agg_ref, grad_ref, back_ref = refs[-4:]
        total = held_ref[...].astype(jnp.float32)
        for ref in refs[1 : 1 + len(arrived)]:
            total = total + ref[...].astype(jnp.float32)
        agg_ref[...] = total.astype(jnp.bfloat16)
        value = jnp.dot(agg_ref[...], weight_ref[...], preferred_element_type=jnp.float32)
        gate, grad = slopes(value, cot_ref[...])
        act_ref[...] = (value * gate).astype(jnp.bfloat16)
        grad_ref[...] = grad
        back_ref[...] = times_transposed(grad, weight_ref[...])

    shapes = [jax.ShapeDtypeStruct((side, n), jnp.bfloat16) for n in (cols, depth, cols, depth)]
    return vmem_call(
        "dense_own",
        kernel,
        shapes,
        (held, *arrived, weight, cotangent),
        flops=4 * side * cols * depth,
        moved=2 * (depth * cols + 6 * side * depth),
    )


def dense_rest(spot, held, arrived, weight, cotangents, agg_own, grad_own):
    rows, depth = held.shape
    side = agg_own.shape[0]
    cols = weight.shape[1]
    part = depth // (rows // side + 1)
    quarter = part // 2

    def kernel(*refs):
        held_ref, weight_ref = refs[0], refs[1 + len(arrived)]
        cot_refs = refs[2 + len(arrived) : 2 + len(arrived) + len(cotangents)]
        agg_ref, grad_ref, near_ref, far_ref, rest_ref, agg, grad = refs[-7:]
        _, group, core = position(spot)
        total = held_ref[...].astype(jnp.float32)
        for ref in refs[1 : 1 + len(arrived)]:
            total = total + ref[...].astype(jnp.float32)
        agg[:side] = agg_ref[...]
        grad[:side] = grad_ref[...]
        agg[side:] = total.astype(jnp.bfloat16)
        value = jnp.dot(agg[side:], weight_ref[...], preferred_element_type=jnp.float32)
        for g, cot_ref in enumerate(cot_refs):
            _, piece = slopes(value[g * side : (g + 1) * side], cot_ref[...])
            grad[(g + 1) * side : (g + 2) * side] = piece
        first = group * part
        far_at = pl.multiple_of(first + (1 - core) * quarter, 128)
        near_at = pl.multiple_of(first + core * quarter, 128)
        far_ref[...] = lax.dot_general(
            agg[:, pl.ds(far_at, quarter)], grad[...], (((0,), (0,)), ((), ())), preferred_element_type=jnp.float32
        ).astype(jnp.bfloat16)
        near_ref[...] = lax.dot_general(
            agg[:, pl.ds(near_at, quarter)], grad[...], (((0,), (0,)), ((), ())), preferred_element_type=jnp.float32
        )
        rest_ref[...] = grad[side:]

    shapes = [
        jax.ShapeDtypeStruct((quarter, cols), jnp.float32),
        jax.ShapeDtypeStruct((quarter, cols), jnp.bfloat16),
        jax.ShapeDtypeStruct((rows, cols), jnp.bfloat16),
    ]
    return vmem_call(
        "dense_rest",
        kernel,
        shapes,
        (held, *arrived, weight, *cotangents, agg_own, grad_own),
        scratch=[pltpu.VMEM((side + rows, depth), jnp.bfloat16), pltpu.VMEM((side + rows, cols), jnp.bfloat16)],
        flops=4 * rows * cols * depth + 2 * (rows + side) * part * cols,
        moved=2 * (depth * cols + 6 * rows * depth),
    )


def back_of(grad, weight):
    def kernel(grad_ref, weight_ref, out_ref):
        out_ref[...] = times_transposed(grad_ref[...], weight_ref[...])

    shape = jax.ShapeDtypeStruct((grad.shape[0], weight.shape[0]), jnp.bfloat16)
    return vmem_call("back_of", kernel, shape, (grad, weight), flops=2 * grad.size * weight.shape[0], moved=2 * weight.size)


def back_blocks(adjacency, parts, count):
    rows, depth = adjacency.shape
    width = parts[0].shape[1]
    height = depth // count

    def kernel(adj_ref, *refs):
        out_refs, held = refs[len(parts) :], refs[-1]
        first = 0
        for ref in refs[: len(parts)]:
            held[first : first + ref.shape[0]] = ref[...]
            first += ref.shape[0]
        for place in reversed(range(count)):
            block = lax.dot_general(
                adj_ref[:, place * height : (place + 1) * height],
                held[...],
                (((0,), (0,)), ((), ())),
                preferred_element_type=jnp.float32,
            ).astype(jnp.bfloat16)
            if place == count - 1:
                out_refs[place][...] = block[:, : width // 2]
                out_refs[place + 1][...] = block[:, width // 2 :]
            else:
                out_refs[place][...] = block

    shapes = [jax.ShapeDtypeStruct((height, width), jnp.bfloat16)] * (count - 1)
    shapes += [jax.ShapeDtypeStruct((height, width // 2), jnp.bfloat16)] * 2
    return vmem_call(
        "back_blocks",
        kernel,
        shapes,
        (adjacency, *parts),
        scratch=[pltpu.VMEM((rows, width), jnp.bfloat16)],
        flops=2 * rows * depth * width,
        moved=2 * (rows * depth + depth * width + rows * width),
    )


def weight_blocks(spot, near, arrived):
    count = len(spot)
    rows, cols = near.shape
    share, middle = rows // count, cols // 2

    def kernel(near_ref, arrived_ref, *refs):
        total = refs[-1]
        me, _, _ = position(spot)
        total[...] = near_ref[...] + arrived_ref[...].astype(jnp.float32)
        for place, away in enumerate(ring_slots(count)):
            at = pl.multiple_of(lax.rem(me + away, count) * share, share)
            block = total[pl.ds(at, share)].astype(jnp.bfloat16)
            if place == count - 1:
                refs[place][...] = block[:, :middle]
                refs[place + 1][...] = block[:, middle:]
            else:
                refs[place][...] = block

    shapes = [jax.ShapeDtypeStruct((share, cols), jnp.bfloat16)] * (count - 1)
    shapes += [jax.ShapeDtypeStruct((share, middle), jnp.bfloat16)] * 2
    scratch = [pltpu.VMEM(near.shape, jnp.float32)]
    return vmem_call("weight_blocks", kernel, shapes, (near, arrived), scratch=scratch, flops=near.size, moved=8 * near.size)


def add_round(sums, carried, after, flops):
    args = [a for entry in sums for a in entry[:2]] + list(carried)

    def kernel(*refs):
        ins, outs = list(refs[: len(args)]), list(refs[len(args) :])
        for _, _, side in sums:
            block, arrived, out = ins.pop(0), ins.pop(0), outs.pop(0)
            width, part = block.shape[1], arrived.shape[1]
            first = (width - part) * side
            if part < width:
                out[...] = block[...]
            out[:, first : first + part] = block[:, first : first + part] + arrived[...]
        for _ in carried:
            outs.pop(0)[...] = ins.pop(0)[...]

    shapes = [jax.ShapeDtypeStruct(entry[0].shape, jnp.bfloat16) for entry in sums]
    shapes += [jax.ShapeDtypeStruct(a.shape, jnp.bfloat16) for a in carried]
    moved = sum(4 * a.size for a in args)
    return vmem_call("add_round", kernel, shapes, args, after=after, flops=flops, moved=moved)


def end_sum(own, first, second, flops):
    def kernel(own_ref, first_ref, second_ref, out_ref):
        total = own_ref[...].astype(jnp.float32) + first_ref[...].astype(jnp.float32) + second_ref[...].astype(jnp.float32)
        out_ref[...] = total.astype(jnp.bfloat16)

    shape = jax.ShapeDtypeStruct(own.shape, jnp.bfloat16)
    return vmem_call("end_sum", kernel, shape, (own, first, second), flops=flops, moved=8 * own.size)


def stack_blocks(blocks, ends=(), after=(), flops=0):
    height, width = (blocks or ends)[0].shape
    if not blocks:
        width *= 2

    def kernel(*refs):
        out_ref = refs[-1]
        for place in range(len(blocks)):
            out_ref[place * height : (place + 1) * height] = refs[place][...]
        for side in range(len(ends)):
            half = width // 2
            out_ref[len(blocks) * height :, side * half : (side + 1) * half] = refs[len(blocks) + side][...]

    total = len(blocks) + len(ends) // 2
    shape = jax.ShapeDtypeStruct((total * height, width), jnp.bfloat16)
    return vmem_call("stack_blocks", kernel, shape, (*blocks, *ends), flops=flops, after=after, moved=4 * total * height * width)


def join_weight(spot, groups, shape, stacks, begun, flops):
    count = len(spot)
    quarter = shape[0] // (2 * groups)
    share = quarter // count
    total = sum(len(s[1]) for s in stacks)
    args = [s[0] for s in stacks]
    out = jax.ShapeDtypeStruct(shape, jnp.float32)
    scratch = [pltpu.VMEM((total, share, shape[1]), jnp.float32), pltpu.SemaphoreType.DMA((total,))]

    def kernel(*refs):
        refs = refs[0 if begun is None else 1 :]
        out_ref, wide, sems = refs[-3:]
        me, group, core = position(spot)
        copies = []
        for ref, (_, aways, steps, other) in zip(refs, stacks):
            back = lax.rem(group + groups - steps, groups)
            base = (back * 2 + (1 - core if other else core)) * quarter
            for place, away in enumerate(aways):
                slot = len(copies)
                wide[slot] = ref[place * share : (place + 1) * share].astype(jnp.float32)
                at = pl.multiple_of(base + lax.rem(me + away, count) * share, share)
                copies.append(pltpu.make_async_copy(wide.at[slot], out_ref.at[pl.ds(at, share)], sems.at[slot]))
                copies[-1].start()
        for copy in copies:
            copy.wait()

    hbm = 0 if begun is None else 1
    return vmem_call(
        "join_weight",
        kernel,
        out,
        [begun] * hbm + args,
        scratch=scratch,
        hbm=hbm,
        hbm_out=True,
        aliases={0: 0} if hbm else None,
        flops=flops,
        moved=6 * total * share * shape[1],
    )


def body(width, feats, weight, tile_vals, tile_rows, tile_cols, tile_count, grad_out):
    count = lax.axis_size("row")
    columns = lax.axis_size("col")
    groups = columns // 2
    rounds = count // 2
    ring = ring_of(count, width)
    spot = [0] * count
    for place, row in enumerate(ring):
        spot[row] = place

    to_right = [(ring[k], ring[(k + 1) % count]) for k in range(count)]
    to_left = [(ring[k], ring[(k - 1) % count]) for k in range(count)]
    swap = [(k, k ^ 1) for k in range(columns)]

    def go(label, right, left):
        with jax.named_scope(label):
            return lax.ppermute(right, "row", to_right), lax.ppermute(left, "row", to_left)

    def go_halves(label, right, left):
        middle = right.shape[1] // 2
        return go(label, right[:, :middle], left[:, middle:])

    def swap_core(label, value):
        with jax.named_scope(label):
            return lax.ppermute(value, "col", swap)

    def from_group(label, value, steps):
        with jax.named_scope(label):
            return lax.ppermute(value, "col", [(k, (k + 2 * steps) % columns) for k in range(columns)])

    adjacency, near_feats = place_tiles(spot, groups, tile_vals, tile_rows, tile_cols, tile_count, feats)
    cotangents = [grad_out] + [from_group("cotangent_y", grad_out, s) for s in range(1, groups)]
    pieces = [near_feats]
    moving = (feats, feats)
    for step in range(1, rounds + 1):
        if step == 2:
            moving = gate(moving, [adjacency])
        if step > 1:
            pieces += moving
        send = go if step < rounds else go_halves
        moving = send(f"feature_ring_{step}", *moving)

    known = aggregate(adjacency, pieces)
    near_own, near_rest, far_own, far_rest = aggregate_last(adjacency, known, moving, feats.shape[0], cotangents[1:])
    rest = (near_rest + swap_core("sum_core_rest", far_rest).astype(jnp.float32)).astype(jnp.bfloat16)
    own = (near_own + swap_core("sum_core_own", far_own).astype(jnp.float32)).astype(jnp.bfloat16)
    side = feats.shape[0]
    parts = [own] + [rest[g * side : (g + 1) * side] for g in range(groups - 1)]
    arrived_own = [from_group(f"sum_y_own_{s}", parts[s], s) for s in range(1, groups)]
    arrived_rest = []
    for s in range(1, groups):
        sent = [parts[(s + g) % groups] for g in range(1, groups)]
        arrived_rest.append(from_group(f"sum_y_rest_{s}", jnp.concatenate(sent) if len(sent) > 1 else sent[0], s))
    activated, agg_own, grad_own, back_own = dense_own(own, arrived_own, weight, cotangents[0])
    turned = [cotangents[groups - g] for g in range(1, groups)]
    near_weight, far_weight, grad_rest = dense_rest(spot, rest, arrived_rest, weight, turned, agg_own, grad_own)

    far_weight = swap_core("weight_core", far_weight)
    back_rest = back_of(grad_rest, weight)
    far_back = [swap_core("back_core_own", back_own), swap_core("back_core_rest", back_rest)]
    terms = weight_blocks(spot, near_weight, far_weight)
    blocks = back_blocks(adjacency, [back_own, back_rest, *far_back], count)
    slots = ring_slots(count)
    starts = [(2 * k * (2 * rounds - 1) + rounds - 1) // (2 * rounds - 2) for k in range(rounds)]
    pieces = []
    weight_moving = [terms[count - 1], terms[count]]
    moving = [blocks[count - 1], blocks[count]]
    early = early_from = None
    ordered = []
    for turn in range(2 * rounds):
        flops = 0 if turn % 2 else LONG
        sums = carried = back_sums = ()
        if 0 < turn < rounds:
            sums = [(terms[2 * (rounds - turn) - side], weight_moving[side], side) for side in range(2)]
        elif turn == rounds:
            weight_moving = [end_sum(terms[0], *weight_moving, flops)] * 2
            pieces.append(weight_moving[0])
        elif turn > rounds:
            carried = weight_moving
            pieces += weight_moving
        begins = turn in starts[1:]
        if begins:
            step = 2 * (rounds - starts.index(turn))
            back_sums = [(blocks[step - side], moving[side], side) for side in range(2)]
        if begins and turn < 2 * rounds - 1:
            apart = turn < rounds
            outs = list(add_round([*sums, *(() if apart else back_sums)], carried, ordered, flops))
            weight_moving = outs[-2:] if sums or carried else weight_moving
            moving = list(add_round(back_sums, (), weight_moving, 0)) if apart else outs[:2]
            ordered = moving[:1] if apart else []
        elif turn > 0 and turn != rounds:
            for side in range(2):
                mine = [*sums[side : side + 1], *back_sums[side : side + 1]]
                outs = add_round(mine, carried[side : side + 1], ordered, flops)
                weight_moving[side] = outs[0] if sums else outs[-1]
                if begins:
                    moving[side] = outs[1] if sums else outs[0]
            ordered = []
        send = go_halves if turn == 2 * rounds - 1 else go
        weight_moving = list(send(f"weight_ring_{turn}", *weight_moving))
        if turn in starts:
            moving = list(go(f"back_ring_{starts.index(turn)}", *moving))
        if turn == 2 * rounds - 2:
            early = stack_blocks(pieces)
            early_from = [from_group(f"weight_y_early_{s}", early, s) for s in range(1, groups)]
    grad_feats = end_sum(blocks[0], *moving, 0)

    late = stack_blocks(pieces[count - 3 :], weight_moving, early_from, LONG)
    late_from = [from_group(f"weight_y_late_{s}", late, s) for s in range(1, groups)]

    def placed(values, steps, part):
        return [
            entry
            for s, value in zip(steps, values)
            for entry in ((value, part, s, False), (swap_core("weight_last", value), part, s, True))
        ]

    along = range(1, groups)
    stacks = placed([early, *early_from], range(groups), slots[: count - 3]) + placed([late], [0], slots[count - 3 :])
    grad_weight = join_weight(spot, groups, weight.shape, stacks, None, LONG)
    grad_weight = join_weight(spot, groups, weight.shape, placed(late_from, along, slots[count - 3 :]), grad_weight, 0)
    return (activated, grad_feats, grad_weight)


def solution(mesh):
    spread = {d.coords[0] for d in mesh.devices.flat if hasattr(d, "coords")}
    placed = (
        P(("row", "col"), None),
        P(),
        P("row", "col", None, None, None),
        P("row", "col", None),
        P("row", "col", None),
        P("row", "col"),
        P(("row", "col"), None),
    )
    return jax.shard_map(
        functools.partial(body, max(1, len(spread))),
        mesh=mesh,
        in_specs=placed,
        out_specs=(P(("row", "col"), None), P(("row", "col"), None), P()),
        check_vma=False,
    )
```

```python
import functools

import jax
import jax.numpy as jnp
from jax import lax
from jax.experimental import pallas as pl
from jax.experimental.pallas import tpu as pltpu
from jax.sharding import PartitionSpec as P

LONG = 20_000_000_000
VMEM_LIMIT = 48 * 1024 * 1024


def ring_of(count, width):
    height = count // width
    if count % width or width % 2 or height < 2:
        return list(range(count))
    walk = [(0, x) for x in range(width)]
    for turn, x in enumerate(reversed(range(width))):
        down = range(1, height) if turn % 2 == 0 else range(height - 1, 0, -1)
        walk += [(z, x) for z in down]
    return [z * width + x for z, x in walk]


def ring_slots(count):
    return [0] + [away for step in range(1, count // 2) for away in (count - step, step)] + [count // 2]


def pick(index, table):
    value = jnp.int32(table[0])
    for at in range(1, len(table)):
        value = jnp.where(index == at, jnp.int32(table[at]), value)
    return value


def position(spot):
    column = lax.axis_index("col")
    return pick(lax.axis_index("row"), spot), lax.div(column, jnp.int32(2)), lax.rem(column, jnp.int32(2))


def vmem_call(name, kernel, out_shapes, args, scratch=(), hbm=0, hbm_out=False, after=(), aliases=None, flops=0, moved=0):
    vmem = pl.BlockSpec(memory_space=pltpu.VMEM)
    anywhere = pl.BlockSpec(memory_space=pl.ANY)
    far = pl.BlockSpec(memory_space=pltpu.HBM)
    specs = [far] * hbm + [vmem] * (len(args) - hbm) + [anywhere] * len(after)
    count = len(args)

    def inner(*refs):
        kernel(*refs[:count], *refs[count + len(after) :])

    return pl.pallas_call(
        inner,
        out_shape=out_shapes,
        in_specs=specs,
        out_specs=jax.tree.map(lambda _: far if hbm_out else vmem, out_shapes),
        scratch_shapes=list(scratch),
        input_output_aliases=aliases or {},
        name=name,
        compiler_params=pltpu.CompilerParams(vmem_limit_bytes=VMEM_LIMIT),
        cost_estimate=pl.CostEstimate(flops=flops, bytes_accessed=moved, transcendentals=0),
    )(*args, *after)


def place_tiles(spot, groups, vals, tile_rows, tile_cols, tile_count, feats):
    slots, side = vals.shape[2], vals.shape[-1]
    count = len(spot)

    def kernel(row_hbm, col_hbm, live_hbm, vals_hbm, feats_hbm, out_ref, feats_ref, row_ref, col_ref, live_ref, held, sems):
        sources = (row_hbm, col_hbm, live_hbm, vals_hbm.at[0, 0], feats_hbm)
        targets = (row_ref, col_ref, live_ref, held, feats_ref)
        copies = [pltpu.make_async_copy(a, b, sems.at[k]) for k, (a, b) in enumerate(zip(sources, targets))]
        for copy in copies:
            copy.start()
        me, group, core = position(spot)
        out_ref[...] = jnp.zeros_like(out_ref)
        for copy in copies:
            copy.wait()

        def put(slot, carry):
            row = row_ref[0, 0, slot]
            other = lax.rem(row, 2) ^ core
            along = lax.rem(lax.div(row, 2) + groups - group, groups)
            top = pl.multiple_of((other * groups + along) * side, side)
            away = lax.rem(pick(col_ref[0, 0, slot], spot) + count - me, count)
            col = jnp.where(away < count // 2, 2 * away, 2 * (count - away) - 1)
            left = pl.multiple_of(col * side, side)
            out_ref[pl.ds(top, side), pl.ds(left, side)] = held[slot]
            return carry

        lax.fori_loop(0, live_ref[0, 0], put, 0)

    shapes = (
        jax.ShapeDtypeStruct((2 * groups * side, count * side), vals.dtype),
        jax.ShapeDtypeStruct(feats.shape, feats.dtype),
    )
    args = (tile_rows, tile_cols, tile_count, vals, feats)
    scratch = [pltpu.SMEM(a.shape, a.dtype) for a in args[:3]]
    scratch += [pltpu.VMEM((slots, side, side), vals.dtype), pltpu.SemaphoreType.DMA((5,))]
    return vmem_call("place_tiles", kernel, shapes, args, scratch=scratch, hbm=5, moved=4 * vals.size)


def gate(values, after):
    def kernel(*refs):
        del refs

    shapes = [jax.ShapeDtypeStruct(v.shape, v.dtype) for v in values]
    return vmem_call("gate", kernel, shapes, values, after=after, aliases={k: k for k in range(len(values))})


def aggregate(adjacency, pieces):
    rows, depth = adjacency.shape
    height, width = pieces[0].shape
    known = len(pieces) * height

    def kernel(*refs):
        adj_ref, out_ref, held = refs[0], refs[-2], refs[-1]
        for place in range(len(pieces)):
            held[place * height : (place + 1) * height] = refs[1 + place][...]
        out_ref[...] = jnp.dot(adj_ref[:, :known], held[...], preferred_element_type=jnp.float32)

    return vmem_call(
        "aggregate",
        kernel,
        jax.ShapeDtypeStruct((rows, width), jnp.float32),
        (adjacency, *pieces),
        scratch=[pltpu.VMEM((known, width), jnp.bfloat16)],
        flops=2 * rows * known * width,
        moved=2 * (rows * depth + known * width + 2 * rows * width),
    )


def aggregate_last(adjacency, known, ends, side, after):
    rows, depth = adjacency.shape
    height, middle = ends[0].shape
    half = rows // 2

    def kernel(adj_ref, known_ref, right_ref, left_ref, near_own, near_rest, far_own, far_rest):
        last = slice(depth - height, depth)
        for first, count, out_ref in (
            (half + side, half - side, far_rest),
            (half, side, far_own),
            (side, half - side, near_rest),
            (0, side, near_own),
        ):
            here = slice(first, first + count)
            for columns, end_ref in ((slice(0, middle), right_ref), (slice(middle, 2 * middle), left_ref)):
                term = jnp.dot(adj_ref[here, last], end_ref[...], preferred_element_type=jnp.float32)
                out_ref[:, columns] = (known_ref[here, columns] + term).astype(out_ref.dtype)

    shapes = [jax.ShapeDtypeStruct((n, 2 * middle), t) for t in (jnp.float32, jnp.bfloat16) for n in (side, half - side)]
    flops = 4 * rows * height * middle
    return vmem_call(
        "aggregate_last", kernel, shapes, (adjacency, known, *ends), after=after, flops=flops, moved=16 * rows * middle
    )


def slopes(value, cotangent):
    gate = jax.nn.sigmoid(value)
    slope = gate * (1.0 + value * (1.0 - gate))
    return gate, (cotangent.astype(jnp.float32) * slope).astype(jnp.bfloat16)


def times_transposed(left, right):
    return lax.dot_general(left, right, (((1,), (1,)), ((), ())), preferred_element_type=jnp.float32).astype(jnp.bfloat16)


def dense_own(held, arrived, weight, cotangent):
    side, depth = held.shape
    cols = weight.shape[1]

    def kernel(*refs):
        held_ref, weight_ref, cot_ref = refs[0], refs[-6], refs[-5]
        act_ref, agg_ref, grad_ref, back_ref = refs[-4:]
        total = held_ref[...].astype(jnp.float32)
        for ref in refs[1 : 1 + len(arrived)]:
            total = total + ref[...].astype(jnp.float32)
        agg_ref[...] = total.astype(jnp.bfloat16)
        value = jnp.dot(agg_ref[...], weight_ref[...], preferred_element_type=jnp.float32)
        gate, grad = slopes(value, cot_ref[...])
        act_ref[...] = (value * gate).astype(jnp.bfloat16)
        grad_ref[...] = grad
        back_ref[...] = times_transposed(grad, weight_ref[...])

    shapes = [jax.ShapeDtypeStruct((side, n), jnp.bfloat16) for n in (cols, depth, cols, depth)]
    return vmem_call(
        "dense_own",
        kernel,
        shapes,
        (held, *arrived, weight, cotangent),
        flops=4 * side * cols * depth,
        moved=2 * (depth * cols + 6 * side * depth),
    )


def dense_rest(spot, held, arrived, weight, cotangents, agg_own, grad_own):
    rows, depth = held.shape
    side = agg_own.shape[0]
    cols = weight.shape[1]
    part = depth // (rows // side + 1)
    quarter = part // 2

    def kernel(*refs):
        held_ref, weight_ref = refs[0], refs[1 + len(arrived)]
        cot_refs = refs[2 + len(arrived) : 2 + len(arrived) + len(cotangents)]
        agg_ref, grad_ref, near_ref, far_ref, rest_ref, agg, grad = refs[-7:]
        _, group, core = position(spot)
        total = held_ref[...].astype(jnp.float32)
        for ref in refs[1 : 1 + len(arrived)]:
            total = total + ref[...].astype(jnp.float32)
        agg[:side] = agg_ref[...]
        grad[:side] = grad_ref[...]
        agg[side:] = total.astype(jnp.bfloat16)
        value = jnp.dot(agg[side:], weight_ref[...], preferred_element_type=jnp.float32)
        for g, cot_ref in enumerate(cot_refs):
            _, piece = slopes(value[g * side : (g + 1) * side], cot_ref[...])
            grad[(g + 1) * side : (g + 2) * side] = piece
        first = group * part
        far_at = pl.multiple_of(first + (1 - core) * quarter, 128)
        near_at = pl.multiple_of(first + core * quarter, 128)
        far_ref[...] = lax.dot_general(
            agg[:, pl.ds(far_at, quarter)], grad[...], (((0,), (0,)), ((), ())), preferred_element_type=jnp.float32
        ).astype(jnp.bfloat16)
        near_ref[...] = lax.dot_general(
            agg[:, pl.ds(near_at, quarter)], grad[...], (((0,), (0,)), ((), ())), preferred_element_type=jnp.float32
        )
        rest_ref[...] = grad[side:]

    shapes = [
        jax.ShapeDtypeStruct((quarter, cols), jnp.float32),
        jax.ShapeDtypeStruct((quarter, cols), jnp.bfloat16),
        jax.ShapeDtypeStruct((rows, cols), jnp.bfloat16),
    ]
    return vmem_call(
        "dense_rest",
        kernel,
        shapes,
        (held, *arrived, weight, *cotangents, agg_own, grad_own),
        scratch=[pltpu.VMEM((side + rows, depth), jnp.bfloat16), pltpu.VMEM((side + rows, cols), jnp.bfloat16)],
        flops=4 * rows * cols * depth + 2 * (rows + side) * part * cols,
        moved=2 * (depth * cols + 6 * rows * depth),
    )


def back_of(grad, weight):
    def kernel(grad_ref, weight_ref, out_ref):
        out_ref[...] = times_transposed(grad_ref[...], weight_ref[...])

    shape = jax.ShapeDtypeStruct((grad.shape[0], weight.shape[0]), jnp.bfloat16)
    return vmem_call("back_of", kernel, shape, (grad, weight), flops=2 * grad.size * weight.shape[0], moved=2 * weight.size)


def back_blocks(adjacency, parts, count):
    rows, depth = adjacency.shape
    width = parts[0].shape[1]
    height = depth // count

    def kernel(adj_ref, *refs):
        out_refs, held = refs[len(parts) :], refs[-1]
        first = 0
        for ref in refs[: len(parts)]:
            held[first : first + ref.shape[0]] = ref[...]
            first += ref.shape[0]
        for place in reversed(range(count)):
            block = lax.dot_general(
                adj_ref[:, place * height : (place + 1) * height],
                held[...],
                (((0,), (0,)), ((), ())),
                preferred_element_type=jnp.float32,
            ).astype(jnp.bfloat16)
            if place == count - 1:
                out_refs[place][...] = block[:, : width // 2]
                out_refs[place + 1][...] = block[:, width // 2 :]
            else:
                out_refs[place][...] = block

    shapes = [jax.ShapeDtypeStruct((height, width), jnp.bfloat16)] * (count - 1)
    shapes += [jax.ShapeDtypeStruct((height, width // 2), jnp.bfloat16)] * 2
    return vmem_call(
        "back_blocks",
        kernel,
        shapes,
        (adjacency, *parts),
        scratch=[pltpu.VMEM((rows, width), jnp.bfloat16)],
        flops=2 * rows * depth * width,
        moved=2 * (rows * depth + depth * width + rows * width),
    )


def weight_blocks(spot, near, arrived):
    count = len(spot)
    rows, cols = near.shape
    share, middle = rows // count, cols // 2

    def kernel(near_ref, arrived_ref, *refs):
        total = refs[-1]
        me, _, _ = position(spot)
        total[...] = near_ref[...] + arrived_ref[...].astype(jnp.float32)
        for place, away in enumerate(ring_slots(count)):
            at = pl.multiple_of(lax.rem(me + away, count) * share, share)
            block = total[pl.ds(at, share)].astype(jnp.bfloat16)
            if place == count - 1:
                refs[place][...] = block[:, :middle]
                refs[place + 1][...] = block[:, middle:]
            else:
                refs[place][...] = block

    shapes = [jax.ShapeDtypeStruct((share, cols), jnp.bfloat16)] * (count - 1)
    shapes += [jax.ShapeDtypeStruct((share, middle), jnp.bfloat16)] * 2
    scratch = [pltpu.VMEM(near.shape, jnp.float32)]
    return vmem_call("weight_blocks", kernel, shapes, (near, arrived), scratch=scratch, flops=near.size, moved=8 * near.size)


def add_round(sums, carried, after, flops):
    args = [a for entry in sums for a in entry[:2]] + list(carried)

    def kernel(*refs):
        ins, outs = list(refs[: len(args)]), list(refs[len(args) :])
        for _, _, side in sums:
            block, arrived, out = ins.pop(0), ins.pop(0), outs.pop(0)
            width, part = block.shape[1], arrived.shape[1]
            first = (width - part) * side
            if part < width:
                out[...] = block[...]
            out[:, first : first + part] = block[:, first : first + part] + arrived[...]
        for _ in carried:
            outs.pop(0)[...] = ins.pop(0)[...]

    shapes = [jax.ShapeDtypeStruct(entry[0].shape, jnp.bfloat16) for entry in sums]
    shapes += [jax.ShapeDtypeStruct(a.shape, jnp.bfloat16) for a in carried]
    moved = sum(4 * a.size for a in args)
    return vmem_call("add_round", kernel, shapes, args, after=after, flops=flops, moved=moved)


def end_sum(own, first, second, flops):
    def kernel(own_ref, first_ref, second_ref, out_ref):
        total = own_ref[...].astype(jnp.float32) + first_ref[...].astype(jnp.float32) + second_ref[...].astype(jnp.float32)
        out_ref[...] = total.astype(jnp.bfloat16)

    shape = jax.ShapeDtypeStruct(own.shape, jnp.bfloat16)
    return vmem_call("end_sum", kernel, shape, (own, first, second), flops=flops, moved=8 * own.size)


def stack_blocks(blocks, ends=(), after=(), flops=0):
    height, width = (blocks or ends)[0].shape
    if not blocks:
        width *= 2

    def kernel(*refs):
        out_ref = refs[-1]
        for place in range(len(blocks)):
            out_ref[place * height : (place + 1) * height] = refs[place][...]
        for side in range(len(ends)):
            half = width // 2
            out_ref[len(blocks) * height :, side * half : (side + 1) * half] = refs[len(blocks) + side][...]

    total = len(blocks) + len(ends) // 2
    shape = jax.ShapeDtypeStruct((total * height, width), jnp.bfloat16)
    return vmem_call("stack_blocks", kernel, shape, (*blocks, *ends), flops=flops, after=after, moved=4 * total * height * width)


def join_weight(spot, groups, shape, stacks, begun, last, flops):
    count = len(spot)
    quarter = shape[0] // (2 * groups)
    share = quarter // count
    total = sum(len(s[1]) for s in stacks)
    args = [s[0] for s in stacks] + list(last)
    outs = [jax.ShapeDtypeStruct(shape, jnp.float32)]
    scratch = [pltpu.VMEM((total, share, shape[1]), jnp.float32), pltpu.SemaphoreType.DMA((total + 1,))]
    if last:
        outs.append(jax.ShapeDtypeStruct(last[0].shape, jnp.bfloat16))
        scratch.append(pltpu.VMEM(last[0].shape, jnp.bfloat16))

    def kernel(*refs):
        refs = refs[0 if begun is None else 1 :]
        out_refs = refs[len(args) : len(args) + len(outs)]
        wide, sems = refs[len(args) + len(outs) : len(args) + len(outs) + 2]
        me, group, core = position(spot)
        copies = []
        for ref, (_, aways, steps, other) in zip(refs, stacks):
            back = lax.rem(group + groups - steps, groups)
            base = (back * 2 + (1 - core if other else core)) * quarter
            for place, away in enumerate(aways):
                slot = len(copies)
                wide[slot] = ref[place * share : (place + 1) * share].astype(jnp.float32)
                at = pl.multiple_of(base + lax.rem(me + away, count) * share, share)
                copies.append(pltpu.make_async_copy(wide.at[slot], out_refs[0].at[pl.ds(at, share)], sems.at[slot]))
                copies[-1].start()
        if last:
            own, first, second = (ref[...].astype(jnp.float32) for ref in refs[len(stacks) : len(args)])
            refs[-1][...] = (own + first + second).astype(jnp.bfloat16)
            copies.append(pltpu.make_async_copy(refs[-1], out_refs[1], sems.at[total]))
            copies[-1].start()
        for copy in copies:
            copy.wait()

    hbm = 0 if begun is None else 1
    return vmem_call(
        "join_weight",
        kernel,
        outs,
        [begun] * hbm + args,
        scratch=scratch,
        hbm=hbm,
        hbm_out=True,
        aliases={0: 0} if hbm else None,
        flops=flops,
        moved=6 * total * share * shape[1],
    )


def body(width, feats, weight, tile_vals, tile_rows, tile_cols, tile_count, grad_out):
    count = lax.axis_size("row")
    columns = lax.axis_size("col")
    groups = columns // 2
    rounds = count // 2
    ring = ring_of(count, width)
    spot = [0] * count
    for place, row in enumerate(ring):
        spot[row] = place

    to_right = [(ring[k], ring[(k + 1) % count]) for k in range(count)]
    to_left = [(ring[k], ring[(k - 1) % count]) for k in range(count)]
    swap = [(k, k ^ 1) for k in range(columns)]

    def go(label, right, left):
        with jax.named_scope(label):
            return lax.ppermute(right, "row", to_right), lax.ppermute(left, "row", to_left)

    def go_halves(label, right, left):
        middle = right.shape[1] // 2
        return go(label, right[:, :middle], left[:, middle:])

    def swap_core(label, value):
        with jax.named_scope(label):
            return lax.ppermute(value, "col", swap)

    def from_group(label, value, steps):
        with jax.named_scope(label):
            return lax.ppermute(value, "col", [(k, (k + 2 * steps) % columns) for k in range(columns)])

    adjacency, near_feats = place_tiles(spot, groups, tile_vals, tile_rows, tile_cols, tile_count, feats)
    cotangents = [grad_out] + [from_group("cotangent_y", grad_out, s) for s in range(1, groups)]
    pieces = [near_feats]
    moving = (feats, feats)
    for step in range(1, rounds + 1):
        if step == 2:
            moving = [gate([value], [adjacency])[0] for value in moving]
        if step > 1:
            pieces += moving
        send = go if step < rounds else go_halves
        moving = send(f"feature_ring_{step}", *moving)

    known = aggregate(adjacency, pieces)
    near_own, near_rest, far_own, far_rest = aggregate_last(adjacency, known, moving, feats.shape[0], cotangents[1:])
    rest = (near_rest + swap_core("sum_core_rest", far_rest).astype(jnp.float32)).astype(jnp.bfloat16)
    own = (near_own + swap_core("sum_core_own", far_own).astype(jnp.float32)).astype(jnp.bfloat16)
    side = feats.shape[0]
    parts = [own] + [rest[g * side : (g + 1) * side] for g in range(groups - 1)]
    arrived_own = [from_group(f"sum_y_own_{s}", parts[s], s) for s in range(1, groups)]
    arrived_rest = []
    for s in range(1, groups):
        sent = [parts[(s + g) % groups] for g in range(1, groups)]
        arrived_rest.append(from_group(f"sum_y_rest_{s}", jnp.concatenate(sent) if len(sent) > 1 else sent[0], s))
    activated, agg_own, grad_own, back_own = dense_own(own, arrived_own, weight, cotangents[0])
    turned = [cotangents[groups - g] for g in range(1, groups)]
    near_weight, far_weight, grad_rest = dense_rest(spot, rest, arrived_rest, weight, turned, agg_own, grad_own)

    far_weight = swap_core("weight_core", far_weight)
    back_rest = back_of(grad_rest, weight)
    far_back = [swap_core("back_core_own", back_own), swap_core("back_core_rest", back_rest)]
    terms = weight_blocks(spot, near_weight, far_weight)
    blocks = back_blocks(adjacency, [back_own, back_rest, *far_back], count)
    slots = ring_slots(count)
    starts = [(2 * k * (2 * rounds - 1) + rounds - 1) // (2 * rounds - 2) for k in range(rounds)]
    pieces = []
    weight_moving = [terms[count - 1], terms[count]]
    moving = [blocks[count - 1], blocks[count]]
    early = early_from = None
    ordered = []
    for turn in range(2 * rounds):
        flops = 0 if turn % 2 else LONG
        sums = carried = back_sums = ()
        if 0 < turn < rounds:
            sums = [(terms[2 * (rounds - turn) - side], weight_moving[side], side) for side in range(2)]
        elif turn == rounds:
            weight_moving = [end_sum(terms[0], *weight_moving, flops)] * 2
            pieces.append(weight_moving[0])
        elif turn > rounds:
            carried = weight_moving
            pieces += weight_moving
        begins = turn in starts[1:]
        if begins:
            step = 2 * (rounds - starts.index(turn))
            back_sums = [(blocks[step - side], moving[side], side) for side in range(2)]
        if begins and turn < 2 * rounds - 1:
            apart = turn < rounds
            outs = list(add_round([*sums, *(() if apart else back_sums)], carried, ordered, flops))
            weight_moving = outs[-2:] if sums or carried else weight_moving
            moving = list(add_round(back_sums, (), weight_moving, 0)) if apart else outs[:2]
            ordered = moving[:1] if apart else []
        elif turn > 0 and turn != rounds:
            for side in range(2):
                mine = [*sums[side : side + 1], *back_sums[side : side + 1]]
                outs = add_round(mine, carried[side : side + 1], ordered, flops)
                weight_moving[side] = outs[0] if sums else outs[-1]
                if begins:
                    moving[side] = outs[1] if sums else outs[0]
            ordered = []
        send = go_halves if turn == 2 * rounds - 1 else go
        weight_moving = list(send(f"weight_ring_{turn}", *weight_moving))
        if turn in starts:
            moving = list(go(f"back_ring_{starts.index(turn)}", *moving))
        if turn == 2 * rounds - 2:
            early = stack_blocks(pieces)
            early_from = [from_group(f"weight_y_early_{s}", early, s) for s in range(1, groups)]

    late = stack_blocks(pieces[count - 3 :], weight_moving, early_from, LONG)
    late_from = [from_group(f"weight_y_late_{s}", late, s) for s in range(1, groups)]

    def placed(values, steps, part):
        return [
            entry
            for s, value in zip(steps, values)
            for entry in ((value, part, s, False), (swap_core("weight_last", value), part, s, True))
        ]

    along = range(1, groups)
    stacks = placed([early, *early_from], range(groups), slots[: count - 3]) + placed([late], [0], slots[count - 3 :])
    grad_weight, grad_feats = join_weight(spot, groups, weight.shape, stacks, None, (blocks[0], *moving), LONG)
    stacks = placed(late_from, along, slots[count - 3 :])
    (grad_weight,) = join_weight(spot, groups, weight.shape, stacks, grad_weight, (), 0)
    return (activated, grad_feats, grad_weight)


def solution(mesh):
    spread = {d.coords[0] for d in mesh.devices.flat if hasattr(d, "coords")}
    placed = (
        P(("row", "col"), None),
        P(),
        P("row", "col", None, None, None),
        P("row", "col", None),
        P("row", "col", None),
        P("row", "col"),
        P(("row", "col"), None),
    )
    return jax.shard_map(
        functools.partial(body, max(1, len(spread))),
        mesh=mesh,
        in_specs=placed,
        out_specs=(P(("row", "col"), None), P(("row", "col"), None), P()),
        check_vma=False,
    )
```

```python
import functools

import jax
import jax.numpy as jnp
from jax import lax
from jax.experimental import pallas as pl
from jax.experimental.pallas import tpu as pltpu
from jax.sharding import PartitionSpec as P

LONG = 20_000_000_000
VMEM_LIMIT = 48 * 1024 * 1024


def ring_of(count, width):
    height = count // width
    if count % width or width % 2 or height < 2:
        return list(range(count))
    walk = [(0, x) for x in range(width)]
    for turn, x in enumerate(reversed(range(width))):
        down = range(1, height) if turn % 2 == 0 else range(height - 1, 0, -1)
        walk += [(z, x) for z in down]
    return [z * width + x for z, x in walk]


def ring_slots(count):
    return [0] + [away for step in range(1, count // 2) for away in (count - step, step)] + [count // 2]


def pick(index, table):
    value = jnp.int32(table[0])
    for at in range(1, len(table)):
        value = jnp.where(index == at, jnp.int32(table[at]), value)
    return value


def position(spot):
    column = lax.axis_index("col")
    return pick(lax.axis_index("row"), spot), lax.div(column, jnp.int32(2)), lax.rem(column, jnp.int32(2))


def vmem_call(name, kernel, out_shapes, args, scratch=(), hbm=0, hbm_out=False, after=(), aliases=None, flops=0, moved=0):
    vmem = pl.BlockSpec(memory_space=pltpu.VMEM)
    anywhere = pl.BlockSpec(memory_space=pl.ANY)
    far = pl.BlockSpec(memory_space=pltpu.HBM)
    specs = [far] * hbm + [vmem] * (len(args) - hbm) + [anywhere] * len(after)
    count = len(args)

    def inner(*refs):
        kernel(*refs[:count], *refs[count + len(after) :])

    return pl.pallas_call(
        inner,
        out_shape=out_shapes,
        in_specs=specs,
        out_specs=jax.tree.map(lambda _: far if hbm_out else vmem, out_shapes),
        scratch_shapes=list(scratch),
        input_output_aliases=aliases or {},
        name=name,
        compiler_params=pltpu.CompilerParams(vmem_limit_bytes=VMEM_LIMIT),
        cost_estimate=pl.CostEstimate(flops=flops, bytes_accessed=moved, transcendentals=0),
    )(*args, *after)


def place_tiles(spot, groups, vals, tile_rows, tile_cols, tile_count, feats):
    slots, side = vals.shape[2], vals.shape[-1]
    count = len(spot)

    def kernel(row_hbm, col_hbm, live_hbm, vals_hbm, feats_hbm, out_ref, feats_ref, row_ref, col_ref, live_ref, held, sems):
        sources = (row_hbm, col_hbm, live_hbm, vals_hbm.at[0, 0], feats_hbm)
        targets = (row_ref, col_ref, live_ref, held, feats_ref)
        copies = [pltpu.make_async_copy(a, b, sems.at[k]) for k, (a, b) in enumerate(zip(sources, targets))]
        for copy in copies:
            copy.start()
        me, group, core = position(spot)
        out_ref[...] = jnp.zeros_like(out_ref)
        for copy in copies:
            copy.wait()

        def put(slot, carry):
            row = row_ref[0, 0, slot]
            other = lax.rem(row, 2) ^ core
            along = lax.rem(lax.div(row, 2) + groups - group, groups)
            top = pl.multiple_of((other * groups + along) * side, side)
            away = lax.rem(pick(col_ref[0, 0, slot], spot) + count - me, count)
            col = jnp.where(away < count // 2, 2 * away, 2 * (count - away) - 1)
            left = pl.multiple_of(col * side, side)
            out_ref[pl.ds(top, side), pl.ds(left, side)] = held[slot]
            return carry

        lax.fori_loop(0, live_ref[0, 0], put, 0)

    shapes = (
        jax.ShapeDtypeStruct((2 * groups * side, count * side), vals.dtype),
        jax.ShapeDtypeStruct(feats.shape, feats.dtype),
    )
    args = (tile_rows, tile_cols, tile_count, vals, feats)
    scratch = [pltpu.SMEM(a.shape, a.dtype) for a in args[:3]]
    scratch += [pltpu.VMEM((slots, side, side), vals.dtype), pltpu.SemaphoreType.DMA((5,))]
    return vmem_call("place_tiles", kernel, shapes, args, scratch=scratch, hbm=5, moved=4 * vals.size)


def gate(values, after):
    def kernel(*refs):
        del refs

    shapes = [jax.ShapeDtypeStruct(v.shape, v.dtype) for v in values]
    return vmem_call("gate", kernel, shapes, values, after=after, aliases={k: k for k in range(len(values))})


def aggregate(adjacency, pieces):
    rows, depth = adjacency.shape
    height, width = pieces[0].shape
    known = len(pieces) * height

    def kernel(*refs):
        adj_ref, out_ref, held = refs[0], refs[-2], refs[-1]
        for place in range(len(pieces)):
            held[place * height : (place + 1) * height] = refs[1 + place][...]
        out_ref[...] = jnp.dot(adj_ref[:, :known], held[...], preferred_element_type=jnp.float32)

    return vmem_call(
        "aggregate",
        kernel,
        jax.ShapeDtypeStruct((rows, width), jnp.float32),
        (adjacency, *pieces),
        scratch=[pltpu.VMEM((known, width), jnp.bfloat16)],
        flops=2 * rows * known * width,
        moved=2 * (rows * depth + known * width + 2 * rows * width),
    )


def aggregate_last(adjacency, known, ends, side, after):
    rows, depth = adjacency.shape
    height, middle = ends[0].shape
    half = rows // 2

    def kernel(adj_ref, known_ref, right_ref, left_ref, near_own, near_rest, far_own, far_rest):
        last = slice(depth - height, depth)
        for first, count, out_ref in (
            (half + side, half - side, far_rest),
            (half, side, far_own),
            (side, half - side, near_rest),
            (0, side, near_own),
        ):
            here = slice(first, first + count)
            for columns, end_ref in ((slice(0, middle), right_ref), (slice(middle, 2 * middle), left_ref)):
                term = jnp.dot(adj_ref[here, last], end_ref[...], preferred_element_type=jnp.float32)
                out_ref[:, columns] = (known_ref[here, columns] + term).astype(out_ref.dtype)

    shapes = [jax.ShapeDtypeStruct((n, 2 * middle), t) for t in (jnp.float32, jnp.bfloat16) for n in (side, half - side)]
    flops = 4 * rows * height * middle
    return vmem_call(
        "aggregate_last", kernel, shapes, (adjacency, known, *ends), after=after, flops=flops, moved=16 * rows * middle
    )


def slopes(value, cotangent):
    gate = jax.nn.sigmoid(value)
    slope = gate * (1.0 + value * (1.0 - gate))
    return gate, (cotangent.astype(jnp.float32) * slope).astype(jnp.bfloat16)


def times_transposed(left, right):
    return lax.dot_general(left, right, (((1,), (1,)), ((), ())), preferred_element_type=jnp.float32).astype(jnp.bfloat16)


def dense_own(held, arrived, weight, cotangent):
    side, depth = held.shape
    cols = weight.shape[1]

    def kernel(*refs):
        held_ref, weight_ref, cot_ref = refs[0], refs[-6], refs[-5]
        act_ref, agg_ref, grad_ref, back_ref = refs[-4:]
        total = held_ref[...].astype(jnp.float32)
        for ref in refs[1 : 1 + len(arrived)]:
            total = total + ref[...].astype(jnp.float32)
        agg_ref[...] = total.astype(jnp.bfloat16)
        value = jnp.dot(agg_ref[...], weight_ref[...], preferred_element_type=jnp.float32)
        gate, grad = slopes(value, cot_ref[...])
        act_ref[...] = (value * gate).astype(jnp.bfloat16)
        grad_ref[...] = grad
        back_ref[...] = times_transposed(grad, weight_ref[...])

    shapes = [jax.ShapeDtypeStruct((side, n), jnp.bfloat16) for n in (cols, depth, cols, depth)]
    return vmem_call(
        "dense_own",
        kernel,
        shapes,
        (held, *arrived, weight, cotangent),
        flops=4 * side * cols * depth,
        moved=2 * (depth * cols + 6 * side * depth),
    )


def dense_rest(spot, held, arrived, weight, cotangents, agg_own, grad_own):
    rows, depth = held.shape
    side = agg_own.shape[0]
    cols = weight.shape[1]
    part = depth // (rows // side + 1)
    quarter = part // 2

    def kernel(*refs):
        held_ref, weight_ref = refs[0], refs[1 + len(arrived)]
        cot_refs = refs[2 + len(arrived) : 2 + len(arrived) + len(cotangents)]
        agg_ref, grad_ref, far_ref, rest_ref, agg, grad = refs[-6:]
        _, group, core = position(spot)
        total = held_ref[...].astype(jnp.float32)
        for ref in refs[1 : 1 + len(arrived)]:
            total = total + ref[...].astype(jnp.float32)
        agg[:side] = agg_ref[...]
        grad[:side] = grad_ref[...]
        agg[side:] = total.astype(jnp.bfloat16)
        value = jnp.dot(agg[side:], weight_ref[...], preferred_element_type=jnp.float32)
        for g, cot_ref in enumerate(cot_refs):
            _, piece = slopes(value[g * side : (g + 1) * side], cot_ref[...])
            grad[(g + 1) * side : (g + 2) * side] = piece
        first = group * part
        far_at = pl.multiple_of(first + (1 - core) * quarter, 128)
        far_ref[...] = lax.dot_general(
            agg[:, pl.ds(far_at, quarter)], grad[...], (((0,), (0,)), ((), ())), preferred_element_type=jnp.float32
        ).astype(jnp.bfloat16)
        rest_ref[...] = grad[side:]

    shapes = [
        jax.ShapeDtypeStruct((quarter, cols), jnp.bfloat16),
        jax.ShapeDtypeStruct((rows, cols), jnp.bfloat16),
        jax.ShapeDtypeStruct((side + rows, depth), jnp.bfloat16),
        jax.ShapeDtypeStruct((side + rows, cols), jnp.bfloat16),
    ]
    return vmem_call(
        "dense_rest",
        kernel,
        shapes,
        (held, *arrived, weight, *cotangents, agg_own, grad_own),
        flops=4 * rows * cols * depth + 2 * (rows + side) * part * cols,
        moved=2 * (depth * cols + 6 * rows * depth),
    )


def own_share(spot, agg, grad, groups):
    depth, cols = agg.shape[1], grad.shape[1]
    quarter = depth // (2 * groups)

    def kernel(agg_ref, grad_ref, out_ref):
        _, group, core = position(spot)
        at = pl.multiple_of((group * 2 + core) * quarter, 128)
        out_ref[...] = lax.dot_general(
            agg_ref[:, pl.ds(at, quarter)], grad_ref[...], (((0,), (0,)), ((), ())), preferred_element_type=jnp.float32
        )

    shape = jax.ShapeDtypeStruct((quarter, cols), jnp.float32)
    return vmem_call("own_share", kernel, shape, (agg, grad), flops=2 * agg.shape[0] * quarter * cols, moved=4 * agg.size)


def back_of(grad, weight):
    def kernel(grad_ref, weight_ref, out_ref):
        out_ref[...] = times_transposed(grad_ref[...], weight_ref[...])

    shape = jax.ShapeDtypeStruct((grad.shape[0], weight.shape[0]), jnp.bfloat16)
    return vmem_call("back_of", kernel, shape, (grad, weight), flops=2 * grad.size * weight.shape[0], moved=2 * weight.size)


def back_blocks(adjacency, parts, count):
    rows, depth = adjacency.shape
    width = parts[0].shape[1]
    height = depth // count

    def kernel(adj_ref, *refs):
        out_refs, held = refs[len(parts) :], refs[-1]
        first = 0
        for ref in refs[: len(parts)]:
            held[first : first + ref.shape[0]] = ref[...]
            first += ref.shape[0]
        for place in reversed(range(count)):
            block = lax.dot_general(
                adj_ref[:, place * height : (place + 1) * height],
                held[...],
                (((0,), (0,)), ((), ())),
                preferred_element_type=jnp.float32,
            ).astype(jnp.bfloat16)
            if place == count - 1:
                out_refs[place][...] = block[:, : width // 2]
                out_refs[place + 1][...] = block[:, width // 2 :]
            else:
                out_refs[place][...] = block

    shapes = [jax.ShapeDtypeStruct((height, width), jnp.bfloat16)] * (count - 1)
    shapes += [jax.ShapeDtypeStruct((height, width // 2), jnp.bfloat16)] * 2
    return vmem_call(
        "back_blocks",
        kernel,
        shapes,
        (adjacency, *parts),
        scratch=[pltpu.VMEM((rows, width), jnp.bfloat16)],
        flops=2 * rows * depth * width,
        moved=2 * (rows * depth + depth * width + rows * width),
    )


def weight_blocks(spot, near, arrived):
    count = len(spot)
    rows, cols = near.shape
    share, middle = rows // count, cols // 2

    def kernel(near_ref, arrived_ref, *refs):
        total = refs[-1]
        me, _, _ = position(spot)
        total[...] = near_ref[...] + arrived_ref[...].astype(jnp.float32)
        for place, away in enumerate(ring_slots(count)):
            at = pl.multiple_of(lax.rem(me + away, count) * share, share)
            block = total[pl.ds(at, share)].astype(jnp.bfloat16)
            if place == count - 1:
                refs[place][...] = block[:, :middle]
                refs[place + 1][...] = block[:, middle:]
            else:
                refs[place][...] = block

    shapes = [jax.ShapeDtypeStruct((share, cols), jnp.bfloat16)] * (count - 1)
    shapes += [jax.ShapeDtypeStruct((share, middle), jnp.bfloat16)] * 2
    scratch = [pltpu.VMEM(near.shape, jnp.float32)]
    return vmem_call("weight_blocks", kernel, shapes, (near, arrived), scratch=scratch, flops=near.size, moved=8 * near.size)


def add_round(sums, carried, after, flops):
    args = [a for entry in sums for a in entry[:2]] + list(carried)

    def kernel(*refs):
        ins, outs = list(refs[: len(args)]), list(refs[len(args) :])
        for _, _, side in sums:
            block, arrived, out = ins.pop(0), ins.pop(0), outs.pop(0)
            width, part = block.shape[1], arrived.shape[1]
            first = (width - part) * side
            if part < width:
                out[...] = block[...]
            out[:, first : first + part] = block[:, first : first + part] + arrived[...]
        for _ in carried:
            outs.pop(0)[...] = ins.pop(0)[...]

    shapes = [jax.ShapeDtypeStruct(entry[0].shape, jnp.bfloat16) for entry in sums]
    shapes += [jax.ShapeDtypeStruct(a.shape, jnp.bfloat16) for a in carried]
    moved = sum(4 * a.size for a in args)
    return vmem_call("add_round", kernel, shapes, args, after=after, flops=flops, moved=moved)


def end_sum(own, first, second, flops):
    def kernel(own_ref, first_ref, second_ref, out_ref):
        total = own_ref[...].astype(jnp.float32) + first_ref[...].astype(jnp.float32) + second_ref[...].astype(jnp.float32)
        out_ref[...] = total.astype(jnp.bfloat16)

    shape = jax.ShapeDtypeStruct(own.shape, jnp.bfloat16)
    return vmem_call("end_sum", kernel, shape, (own, first, second), flops=flops, moved=8 * own.size)


def stack_blocks(blocks, ends=(), after=(), flops=0):
    height, width = (blocks or ends)[0].shape
    if not blocks:
        width *= 2

    def kernel(*refs):
        out_ref = refs[-1]
        for place in range(len(blocks)):
            out_ref[place * height : (place + 1) * height] = refs[place][...]
        for side in range(len(ends)):
            half = width // 2
            out_ref[len(blocks) * height :, side * half : (side + 1) * half] = refs[len(blocks) + side][...]

    total = len(blocks) + len(ends) // 2
    shape = jax.ShapeDtypeStruct((total * height, width), jnp.bfloat16)
    return vmem_call("stack_blocks", kernel, shape, (*blocks, *ends), flops=flops, after=after, moved=4 * total * height * width)


def join_weight(spot, groups, shape, stacks, begun, last, flops):
    count = len(spot)
    quarter = shape[0] // (2 * groups)
    share = quarter // count
    total = sum(len(s[1]) for s in stacks)
    args = [s[0] for s in stacks] + list(last)
    outs = [jax.ShapeDtypeStruct(shape, jnp.float32)]
    scratch = [pltpu.VMEM((total, share, shape[1]), jnp.float32), pltpu.SemaphoreType.DMA((total + 1,))]
    if last:
        outs.append(jax.ShapeDtypeStruct(last[0].shape, jnp.bfloat16))
        scratch.append(pltpu.VMEM(last[0].shape, jnp.bfloat16))

    def kernel(*refs):
        refs = refs[0 if begun is None else 1 :]
        out_refs = refs[len(args) : len(args) + len(outs)]
        wide, sems = refs[len(args) + len(outs) : len(args) + len(outs) + 2]
        me, group, core = position(spot)
        copies = []
        for ref, (_, aways, steps, other) in zip(refs, stacks):
            back = lax.rem(group + groups - steps, groups)
            base = (back * 2 + (1 - core if other else core)) * quarter
            for place, away in enumerate(aways):
                slot = len(copies)
                wide[slot] = ref[place * share : (place + 1) * share].astype(jnp.float32)
                at = pl.multiple_of(base + lax.rem(me + away, count) * share, share)
                copies.append(pltpu.make_async_copy(wide.at[slot], out_refs[0].at[pl.ds(at, share)], sems.at[slot]))
                copies[-1].start()
        if last:
            own, first, second = (ref[...].astype(jnp.float32) for ref in refs[len(stacks) : len(args)])
            refs[-1][...] = (own + first + second).astype(jnp.bfloat16)
            copies.append(pltpu.make_async_copy(refs[-1], out_refs[1], sems.at[total]))
            copies[-1].start()
        for copy in copies:
            copy.wait()

    hbm = 0 if begun is None else 1
    return vmem_call(
        "join_weight",
        kernel,
        outs,
        [begun] * hbm + args,
        scratch=scratch,
        hbm=hbm,
        hbm_out=True,
        aliases={0: 0} if hbm else None,
        flops=flops,
        moved=6 * total * share * shape[1],
    )


def body(width, feats, weight, tile_vals, tile_rows, tile_cols, tile_count, grad_out):
    count = lax.axis_size("row")
    columns = lax.axis_size("col")
    groups = columns // 2
    rounds = count // 2
    ring = ring_of(count, width)
    spot = [0] * count
    for place, row in enumerate(ring):
        spot[row] = place

    to_right = [(ring[k], ring[(k + 1) % count]) for k in range(count)]
    to_left = [(ring[k], ring[(k - 1) % count]) for k in range(count)]
    swap = [(k, k ^ 1) for k in range(columns)]

    def go(label, right, left):
        with jax.named_scope(label):
            return lax.ppermute(right, "row", to_right), lax.ppermute(left, "row", to_left)

    def go_halves(label, right, left):
        middle = right.shape[1] // 2
        return go(label, right[:, :middle], left[:, middle:])

    def swap_core(label, value):
        with jax.named_scope(label):
            return lax.ppermute(value, "col", swap)

    def from_group(label, value, steps):
        with jax.named_scope(label):
            return lax.ppermute(value, "col", [(k, (k + 2 * steps) % columns) for k in range(columns)])

    adjacency, near_feats = place_tiles(spot, groups, tile_vals, tile_rows, tile_cols, tile_count, feats)
    cotangents = [grad_out] + [from_group("cotangent_y", grad_out, s) for s in range(1, groups)]
    pieces = [near_feats]
    moving = (feats, feats)
    for step in range(1, rounds + 1):
        if step == 2:
            moving = [gate([value], [adjacency])[0] for value in moving]
        if step > 1:
            pieces += moving
        send = go if step < rounds else go_halves
        moving = send(f"feature_ring_{step}", *moving)

    known = aggregate(adjacency, pieces)
    near_own, near_rest, far_own, far_rest = aggregate_last(adjacency, known, moving, feats.shape[0], cotangents[1:])
    rest = (near_rest + swap_core("sum_core_rest", far_rest).astype(jnp.float32)).astype(jnp.bfloat16)
    own = (near_own + swap_core("sum_core_own", far_own).astype(jnp.float32)).astype(jnp.bfloat16)
    side = feats.shape[0]
    parts = [own] + [rest[g * side : (g + 1) * side] for g in range(groups - 1)]
    arrived_own = [from_group(f"sum_y_own_{s}", parts[s], s) for s in range(1, groups)]
    arrived_rest = []
    for s in range(1, groups):
        sent = [parts[(s + g) % groups] for g in range(1, groups)]
        arrived_rest.append(from_group(f"sum_y_rest_{s}", jnp.concatenate(sent) if len(sent) > 1 else sent[0], s))
    activated, agg_own, grad_own, back_own = dense_own(own, arrived_own, weight, cotangents[0])
    turned = [cotangents[groups - g] for g in range(1, groups)]
    far_weight, grad_rest, agg, grad = dense_rest(spot, rest, arrived_rest, weight, turned, agg_own, grad_own)

    near_weight = own_share(spot, agg, grad, groups)
    far_weight = swap_core("weight_core", far_weight)
    back_rest = back_of(grad_rest, weight)
    far_back = [swap_core("back_core_own", back_own), swap_core("back_core_rest", back_rest)]
    terms = weight_blocks(spot, near_weight, far_weight)
    blocks = back_blocks(adjacency, [back_own, back_rest, *far_back], count)
    slots = ring_slots(count)
    starts = [(2 * k * (2 * rounds - 1) + rounds - 1) // (2 * rounds - 2) for k in range(rounds)]
    pieces = []
    weight_moving = [terms[count - 1], terms[count]]
    moving = [blocks[count - 1], blocks[count]]
    early = early_from = None
    ordered = []
    for turn in range(2 * rounds):
        flops = 0 if turn % 2 else LONG
        sums = carried = back_sums = ()
        if 0 < turn < rounds:
            sums = [(terms[2 * (rounds - turn) - side], weight_moving[side], side) for side in range(2)]
        elif turn == rounds:
            weight_moving = [end_sum(terms[0], *weight_moving, flops)] * 2
            pieces.append(weight_moving[0])
        elif turn > rounds:
            carried = weight_moving
            pieces += weight_moving
        begins = turn in starts[1:]
        if begins:
            step = 2 * (rounds - starts.index(turn))
            back_sums = [(blocks[step - side], moving[side], side) for side in range(2)]
        if begins and turn < 2 * rounds - 1:
            apart = turn < rounds
            outs = list(add_round([*sums, *(() if apart else back_sums)], carried, ordered, flops))
            weight_moving = outs[-2:] if sums or carried else weight_moving
            moving = list(add_round(back_sums, (), weight_moving, 0)) if apart else outs[:2]
            ordered = moving[:1] if apart else []
        elif turn > 0 and turn != rounds:
            for side in range(2):
                mine = [*sums[side : side + 1], *back_sums[side : side + 1]]
                outs = add_round(mine, carried[side : side + 1], ordered, flops)
                weight_moving[side] = outs[0] if sums else outs[-1]
                if begins:
                    moving[side] = outs[1] if sums else outs[0]
            ordered = []
        send = go_halves if turn == 2 * rounds - 1 else go
        weight_moving = list(send(f"weight_ring_{turn}", *weight_moving))
        if turn in starts:
            moving = list(go(f"back_ring_{starts.index(turn)}", *moving))
        if turn == 2 * rounds - 2:
            early = stack_blocks(pieces)
            early_from = [from_group(f"weight_y_early_{s}", early, s) for s in range(1, groups)]

    late = stack_blocks(pieces[count - 3 :], weight_moving, early_from, LONG)
    late_from = [from_group(f"weight_y_late_{s}", late, s) for s in range(1, groups)]

    def placed(values, steps, part):
        return [
            entry
            for s, value in zip(steps, values)
            for entry in ((value, part, s, False), (swap_core("weight_last", value), part, s, True))
        ]

    along = range(1, groups)
    stacks = placed([early, *early_from], range(groups), slots[: count - 3]) + placed([late], [0], slots[count - 3 :])
    grad_weight, grad_feats = join_weight(spot, groups, weight.shape, stacks, None, (blocks[0], *moving), LONG)
    stacks = placed(late_from, along, slots[count - 3 :])
    (grad_weight,) = join_weight(spot, groups, weight.shape, stacks, grad_weight, (), 0)
    return (activated, grad_feats, grad_weight)


def solution(mesh):
    spread = {d.coords[0] for d in mesh.devices.flat if hasattr(d, "coords")}
    placed = (
        P(("row", "col"), None),
        P(),
        P("row", "col", None, None, None),
        P("row", "col", None),
        P("row", "col", None),
        P("row", "col"),
        P(("row", "col"), None),
    )
    return jax.shard_map(
        functools.partial(body, max(1, len(spread))),
        mesh=mesh,
        in_specs=placed,
        out_specs=(P(("row", "col"), None), P(("row", "col"), None), P()),
        check_vma=False,
    )
```
